512 devices in a mesh: prow: 32 (over x, z_lo), pcol: 16 (over z_hi, y, core).
Axes of the slice: x: 4, y: 4, z: 16 (z_hi: 2, z_lo: 8; z = z_hi * 8 + z_lo), core: 2. Of those that a mesh axis runs over, the one named last changes fastest.
Arguments:
- inverse_part: float32 [12288, 12288], P('prow', 'pcol'), may hold values from -0.0546875 to 0.0546875
- lower_panel: float32 [12288, 2048], P('prow', 'pcol'), may hold values from -2 to 2
- struct_mask: int32 [16, 96], P('pcol', 'prow'), may hold values 0 or 1
- diag_inverse: float32 [16, 128, 128], P('pcol'), may hold values from -6 to 6
Outputs:
- off_diag: float32 [12288, 2048], P('prow', 'pcol')
- diag_block: float32 [16, 128, 128], P('pcol')
The draws below stay inside these ranges and needn't reach their ends.
All inputs are finite; a program needn't handle non-finite values. No bound on the sum of `struct_mask` on one device may be relied on, other than what follows from the above.
Results may differ from the reference program's by a relative error of at most 0.00007.
Values sent between devices are 32-bit elements; how exact they have to be, the bound alone decides.
A program may use at most 64 MiB of HBM per device.

```python
import jax
import jax.numpy as jnp
from jax import lax

BLK = 128
NT = 96
KS = 16


def with_ends(result, own_key, smallest, high):
    longest = result.shape.index(max(result.shape))
    spots = []
    for shift in (0, 1):
        where = [jax.random.randint(jax.random.fold_in(own_key, axis), (), 0, length) for axis, length in enumerate(result.shape)]
        where[longest] = (where[longest] + shift) % result.shape[longest]
        spots.append(tuple(where))
    return result.at[spots[0]].set(smallest).at[spots[1]].set(high)


def block_scale(stream_key, extent, split, smallest, top_value):
    loudness, own = 1.0, jax.random.fold_in(stream_key, 6)
    for dim, shards_of in split:
        draws = jnp.exp(jax.random.uniform(jax.random.fold_in(own, dim), (shards_of,), jnp.float32, smallest / len(split), top_value / len(split)))
        loudness = loudness * jnp.repeat(draws, extent[dim] // shards_of).reshape([-1 if axis == dim else 1 for axis in range(len(extent))])
    return loudness


def gaussian(rng, shape, deviation, limit, split=(), kind=jnp.bfloat16):
    array = jax.random.normal(rng, shape, jnp.float32) * deviation
    if len(split) > 0:
        array = block_scale(rng, shape, split, -0.22, 0.18) * array
    return jnp.clip(array, min=-limit, max=limit).astype(kind)


def setup_inputs(seed: int = 0) -> dict:
    streams_of = jax.random.split(jax.random.key(seed), 5)
    inverse_part = gaussian(streams_of[0], (NT * BLK, NT * BLK), (NT * BLK) ** -0.5, 0.0546875, ((0, 32), (1, 16)), jnp.float32)
    lower_panel = gaussian(streams_of[1], (NT * BLK, KS * BLK), 0.3, 2.0, ((0, 32), (1, 16)), jnp.float32)
    struct_mask = with_ends((jax.random.randint(streams_of[2], (KS, NT), 0, 2) < 1).astype(jnp.int32), jax.random.fold_in(streams_of[2], 1), 0, 1)
    diag_inverse = gaussian(streams_of[3], (KS, BLK, BLK), 1.0, 6.0, ((0, 16),), jnp.float32)
    return {"inverse_part": inverse_part, "lower_panel": lower_panel, "struct_mask": struct_mask, "diag_inverse": diag_inverse}


def reference(inverse_part, lower_panel, struct_mask, diag_inverse):
    member = jnp.transpose(struct_mask).astype(jnp.float32)
    masked = (lower_panel.reshape(NT, BLK, KS, BLK) * member[:, None, :, None]).reshape(NT * BLK, KS * BLK)
    product = jnp.dot(inverse_part, masked, precision=lax.Precision.HIGHEST, preferred_element_type=jnp.float32)
    off_diag = -(product.reshape(NT, BLK, KS, BLK) * member[:, None, :, None]).reshape(NT * BLK, KS * BLK)
    correction = jnp.einsum("ika,ikb->kab", masked.reshape(NT * BLK, KS, BLK), off_diag.reshape(NT * BLK, KS, BLK), precision=lax.Precision.HIGHEST)
    diag_block = diag_inverse - correction
    return off_diag, diag_block
```

```python
import jax
import jax.numpy as jnp
from jax import lax
from jax.experimental import pallas as pl
from jax.experimental.pallas import tpu as pltpu
from jax.sharding import PartitionSpec as P

MESH = pl.DeviceIdType.MESH
X, ZL, ZH, Y = 4, 8, 2, 4
PIECES = 3
LAG = 4
LEAD = 2
TRAIL = 2


def split(value):
    high = value.astype(jnp.bfloat16)
    return high, (value - high.astype(jnp.float32)).astype(jnp.bfloat16)


def product(left_high, left_low, right):
    high, low = split(right)
    width = right.shape[1]
    both = jnp.dot(
        left_high, jnp.concatenate([high, low], axis=1), preferred_element_type=jnp.float32
    )
    rest = jnp.dot(left_low, high, preferred_element_type=jnp.float32)
    return both[:, :width] + (both[:, width:] + rest)


def copy_to(src, dst, send, recv, device):
    return pltpu.make_async_remote_copy(
        src_ref=src, dst_ref=dst, send_sem=send, recv_sem=recv,
        device_id=device, device_id_type=MESH,
    )


def kernel(
    a_hbm, l_hbm, mask_ref, dinv_hbm, off_ref, diag_ref,
    a_ref, l_ref, dinv_ref, masked, turned, a_in, a_high, a_low, m, p, c, yr, t, zb, cs, cx, cz, dg,
    fetch, s_a, r_a, s_first, s_right, s_left, s_x, r_m, s_c, r_c, s_y, r_y, s_z, r_z,
    s_cx, r_cx, s_cz, r_cz, s_dg, r_dg,
):
    row, col = lax.axis_index("prow"), lax.axis_index("pcol")
    x, zl = lax.div(row, ZL), lax.rem(row, ZL)
    zh, y, co = lax.div(col, 8), lax.rem(lax.div(col, 2), Y), lax.rem(col, 2)

    def device(x, zl, zh, y, co):
        return (x * ZL + zl, zh * 8 + y * 2 + co)

    kind = lax.rem(lax.div(x + 1, 2), 2)
    x_a, x_m = x + 1 - 2 * lax.rem(x, 2), 3 - x
    home = co == kind
    mine = lax.rem(lax.div(x, 2) + zh, 2)

    first_to = device(
        lax.rem(zl + lax.div(x, 2), 2) * 2 + lax.rem(lax.rem(zl + lax.div(x, 2), 2) + co, 2),
        2 * y + 1 - zh,
        lax.div(x, 2), 2 * lax.rem(x, 2) + lax.div(zl, 4), lax.rem(lax.div(zl, 2), 2),
    )
    first_slot = 2 * y + 1 - zh
    first_half = lax.rem(zl, 2)
    first_from = device(
        2 * zh + lax.div(y, 2),
        4 * lax.rem(y, 2) + 2 * co + mine,
        1 - lax.rem(zl, 2), lax.div(zl, 2), kind,
    )
    sibling = device(x, zl, zh, y, 1 - co)
    partner = device(x_m, zl, zh, y, co)
    a_partner = device(x_a, zl, zh, y, co)

    def x_peer(step):
        return device(lax.rem(x + step, X), zl, zh, y, co)

    def z_peer(step):
        return device(x, lax.rem(zl + step, ZL), zh, y, co)

    def y_peer(step):
        return device(x, zl, zh, lax.rem(y + step, Y), co)

    def end_peer(half):
        return device(jnp.where(home, x, x_a), zl, half, y, kind)

    fetch_l = pltpu.make_async_copy(l_hbm, l_ref, fetch.at[0])
    fetch_a = pltpu.make_async_copy(a_hbm, a_ref, fetch.at[1])
    fetch_dinv = pltpu.make_async_copy(dinv_hbm, dinv_ref, fetch.at[2])
    fetch_l.start()
    fetch_a.start()
    fetch_dinv.start()

    barrier = pltpu.get_barrier_semaphore()

    def greet(who):
        pl.semaphore_signal(barrier, inc=1, device_id=who, device_id_type=MESH)

    greet(first_from)
    greet(sibling)
    for step in range(1, X):
        greet(x_peer(step))
    for step in range(1, Y):
        greet(y_peer(step))
    for step in range(1, ZL):
        greet(z_peer(step))
    greet(end_peer(1 - zh))

    @pl.when(jnp.logical_not(home))
    def _():
        greet(end_peer(zh))

    fetch_l.wait()
    for block in range(3):
        rows = pl.ds(block * 128, 128)
        member = mask_ref[0, block].astype(jnp.float32)
        masked[rows, :] = l_ref[rows, :] * member

    pl.semaphore_wait(barrier, jnp.where(home, 16, 17))

    first = copy_to(
        masked, m.at[first_slot, first_half], s_first, r_m.at[first_slot, first_half], first_to
    )
    first.start()

    def send_a(piece):
        rows = pl.ds(piece * 128, 128)
        return copy_to(
            a_ref.at[rows, :], a_in.at[rows, :], s_a.at[piece], r_a.at[piece], a_partner
        )

    fetch_a.wait()
    high, low = split(a_ref[...])
    a_high[kind], a_low[kind] = high, low
    high, low = split(masked[...].T)
    turned[0], turned[1] = high, low

    def order(i):
        half = lax.div(i + 1, 2)
        near = jnp.where(lax.rem(i, 2) == 1, zl - half, zl + half)
        far = jnp.where(zl <= 3, i, 7 - i)
        return jnp.where(i <= 2 * jnp.minimum(zl, 7 - zl), near, far)

    def to_right(j):
        return copy_to(
            m.at[j, mine], m.at[j, mine], s_right.at[j], r_m.at[j, mine],
            device(x, jnp.minimum(zl + 1, 7), zh, y, co),
        )

    def to_left(j):
        return copy_to(
            m.at[j, mine], m.at[j, mine], s_left.at[j], r_m.at[j, mine],
            device(x, jnp.maximum(zl - 1, 0), zh, y, co),
        )

    def to_partner(j):
        return copy_to(m.at[j, mine], m.at[j, mine], s_x.at[j], r_m.at[j, mine], partner)

    def arrival(j, half):
        return copy_to(m.at[j, half], m.at[j, half], s_first, r_m.at[j, half], partner)

    def to_sibling(j):
        return copy_to(p.at[j, 1 - co], c.at[j], s_c.at[j], r_c.at[j], sibling)

    def to_owner(j):
        owner = lax.div(j, 2)
        slot = lax.rem(y - owner + Y, Y) - 1
        half = 1 - lax.rem(j, 2)
        return copy_to(
            p.at[j, co], yr.at[half, slot], s_y.at[j], r_y.at[half, slot],
            device(x, zl, zh, owner, co),
        )

    def to_end(half):
        return copy_to(t.at[half], zb.at[zh], s_z.at[half], r_z.at[zh], end_peer(half))

    def goes_right(j):
        return jnp.logical_and(j <= zl, zl < 7)

    def goes_left(j):
        return jnp.logical_and(j >= zl, zl > 0)

    def part(j, q):
        p[j, q] = product(a_high[q], a_low[q], m[j].reshape(768, 128))

    def step(i, carry):
        @pl.when(i < 8)
        def _():
            j = order(i)
            arrival(j, mine).wait_recv()
            to_partner(j).start()

            @pl.when(goes_right(j))
            def _():
                to_right(j).start()

            @pl.when(goes_left(j))
            def _():
                to_left(j).start()

        for piece in range(PIECES):

            @pl.when(i == piece)
            def _(piece=piece):
                send_a(piece).start()

        @pl.when(jnp.logical_and(i >= LEAD, i < LEAD + 8))
        def _():
            j = order(i - LEAD)
            arrival(j, 1 - mine).wait_recv()
            part(j, kind)

            @pl.when(jnp.logical_not(home))
            def _():
                to_sibling(j).start()

        @pl.when(i == LAG)
        def _():
            for piece in range(PIECES):
                send_a(piece).wait_recv()
            high, low = split(a_in[...])
            a_high[1 - kind], a_low[1 - kind] = high, low

        @pl.when(jnp.logical_and(i >= LAG, i < LAG + 8))
        def _():
            j = order(i - LAG)
            part(j, 1 - kind)

            @pl.when(home)
            def _():
                to_sibling(j).start()

        k = i - jnp.where(home, LEAD + 1, LAG + 1)

        @pl.when(jnp.logical_and(k >= 0, k < 8))
        def _():
            j = order(k)
            to_sibling(j).wait_recv()
            p[j, co] = p[j, co] + c[j]

            @pl.when(lax.div(j, 2) != y)
            def _():
                to_owner(j).start()

        @pl.when(jnp.logical_and(k >= TRAIL, k < TRAIL + 8))
        def _():
            j = order(k - TRAIL)
            half = 1 - lax.rem(j, 2)

            @pl.when(lax.div(j, 2) == y)
            def _():
                for slot in range(3):
                    copy_to(
                        t.at[0], yr.at[half, slot], s_y.at[0], r_y.at[half, slot], sibling
                    ).wait_recv()
                total = (p[j, co] + yr[half, 0]) + (yr[half, 1] + yr[half, 2])
                stays = jnp.logical_and(home, half == zh)

                @pl.when(stays)
                def _():
                    zb[zh] = total

                @pl.when(jnp.logical_not(stays))
                def _():
                    t[half] = total
                    to_end(half).start()

        return carry

    lax.fori_loop(0, 8 + LAG + 1 + TRAIL, step, 0)

    def end_arrival(half):
        return copy_to(t.at[0], zb.at[half], s_z.at[0], r_z.at[half], sibling)

    end_arrival(1 - zh).wait_recv()

    @pl.when(jnp.logical_not(home))
    def _():
        end_arrival(zh).wait_recv()

    for block in range(3):
        rows = pl.ds(block * 128, 128)
        member = mask_ref[0, block].astype(jnp.float32)
        off_ref[rows, :] = -((zb[0, rows, :] + zb[1, rows, :]) * member)

    correction = product(turned[0], turned[1], off_ref[...])
    for other in range(X):
        cs[other] = correction[other * 32 : other * 32 + 32, :]

    def corr_x(step):
        return copy_to(
            cs.at[lax.rem(x + step, X)], cx.at[step - 1], s_cx.at[step - 1], r_cx.at[step - 1],
            x_peer(step),
        )

    def corr_z(step):
        return copy_to(cz.at[zl], cz.at[zl], s_cz.at[step - 1], r_cz.at[zl], z_peer(step))

    def corr_back(step):
        return copy_to(dg.at[x], dg.at[x], s_dg.at[step - 1], r_dg.at[x], x_peer(step))

    for step_ in range(1, X):
        corr_x(step_).start()
    for step_ in range(1, X):
        corr_x(step_).wait_recv()
    cz[zl] = (cs[x] + cx[0]) + (cx[1] + cx[2])
    for step_ in range(1, ZL):
        corr_z(step_).start()
    for step_ in range(1, ZL):
        other = lax.rem(zl + step_, ZL)
        copy_to(cz.at[other], cz.at[other], s_cz.at[0], r_cz.at[other], sibling).wait_recv()
    dg[x] = ((cz[0] + cz[1]) + (cz[2] + cz[3])) + ((cz[4] + cz[5]) + (cz[6] + cz[7]))
    for step_ in range(1, X):
        corr_back(step_).start()
    for step_ in range(1, X):
        other = lax.rem(x + step_, X)
        copy_to(dg.at[other], dg.at[other], s_dg.at[0], r_dg.at[other], sibling).wait_recv()
    fetch_dinv.wait()
    for other in range(X):
        rows = pl.ds(other * 32, 32)
        diag_ref[0, rows, :] = dinv_ref[0, rows, :] - dg[other]

    first.wait_send()
    for piece in range(PIECES):
        send_a(piece).wait_send()

    def finish(j, carry):
        to_partner(j).wait_send()
        to_sibling(j).wait_send()

        @pl.when(goes_right(j))
        def _():
            to_right(j).wait_send()

        @pl.when(goes_left(j))
        def _():
            to_left(j).wait_send()

        @pl.when(lax.div(j, 2) != y)
        def _():
            to_owner(j).wait_send()

        return carry

    lax.fori_loop(0, 8, finish, 0)
    to_end(1 - zh).wait_send()

    @pl.when(jnp.logical_not(home))
    def _():
        to_end(zh).wait_send()

    for step_ in range(1, X):
        corr_x(step_).wait_send()
        corr_back(step_).wait_send()
    for step_ in range(1, ZL):
        corr_z(step_).wait_send()


def on_device(inverse_part, lower_panel, struct_mask, diag_inverse):
    f32, bf16 = jnp.float32, jnp.bfloat16
    dma = pltpu.SemaphoreType.DMA
    hbm = pl.BlockSpec(memory_space=pl.ANY)
    vmem = pl.BlockSpec(memory_space=pltpu.VMEM)
    return tuple(
        pl.pallas_call(
            kernel,
            out_shape=(
                jax.ShapeDtypeStruct((384, 128), f32),
                jax.ShapeDtypeStruct((1, 128, 128), f32),
            ),
            in_specs=[hbm, hbm, pl.BlockSpec(memory_space=pltpu.SMEM), hbm],
            out_specs=(vmem, vmem),
            scratch_shapes=[
                pltpu.VMEM((384, 768), f32),
                pltpu.VMEM((384, 128), f32),
                pltpu.VMEM((1, 128, 128), f32),
                pltpu.VMEM((384, 128), f32),
                pltpu.VMEM((2, 128, 384), bf16),
                pltpu.VMEM((384, 768), f32),
                pltpu.VMEM((2, 384, 768), bf16),
                pltpu.VMEM((2, 384, 768), bf16),
                pltpu.VMEM((8, 2, 384, 128), f32),
                pltpu.VMEM((8, 2, 384, 128), f32),
                pltpu.VMEM((8, 384, 128), f32),
                pltpu.VMEM((2, 3, 384, 128), f32),
                pltpu.VMEM((2, 384, 128), f32),
                pltpu.VMEM((2, 384, 128), f32),
                pltpu.VMEM((4, 32, 128), f32),
                pltpu.VMEM((3, 32, 128), f32),
                pltpu.VMEM((8, 32, 128), f32),
                pltpu.VMEM((4, 32, 128), f32),
                dma((3,)), dma((PIECES,)), dma((PIECES,)), dma,
                dma((8,)), dma((8,)), dma((8,)), dma((8, 2)),
                dma((8,)), dma((8,)), dma((8,)), dma((2, 3)), dma((2,)), dma((2,)),
                dma((3,)), dma((3,)), dma((7,)), dma((8,)), dma((3,)), dma((4,)),
            ],
            compiler_params=pltpu.CompilerParams(
                collective_id=0, has_side_effects=True, vmem_limit_bytes=48 * 1024 * 1024
            ),
            cost_estimate=pl.CostEstimate(
                flops=2 * 3 * 384 * 768 * 2048, bytes_accessed=4_000_000, transcendentals=0
            ),
        )(inverse_part, lower_panel, struct_mask, diag_inverse)
    )


def solution(mesh):
    return jax.shard_map(
        on_device,
        mesh=mesh,
        in_specs=(P("prow", "pcol"), P("prow", "pcol"), P("pcol", "prow"), P("pcol", None, None)),
        out_specs=(P("prow", "pcol"), P("pcol", None, None)),
        check_vma=False,
    )
```

```python
import jax
import jax.numpy as jnp
from jax import lax
from jax.experimental import pallas as pl
from jax.experimental.pallas import tpu as pltpu
from jax.sharding import PartitionSpec as P

MESH = pl.DeviceIdType.MESH
X, ZL, ZH, Y = 4, 8, 2, 4
PIECES = 3
PARTS = 2
LAG = 6
LEAD = 2
TRAIL = 3


def split(value):
    high = value.astype(jnp.bfloat16)
    return high, (value - high.astype(jnp.float32)).astype(jnp.bfloat16)


def product(left_high, left_low, right):
    high, low = split(right)
    width = right.shape[1]
    both = jnp.dot(
        left_high, jnp.concatenate([high, low], axis=1), preferred_element_type=jnp.float32
    )
    rest = jnp.dot(left_low, high, preferred_element_type=jnp.float32)
    return both[:, :width] + (both[:, width:] + rest)


def copy_to(src, dst, send, recv, device):
    return pltpu.make_async_remote_copy(
        src_ref=src, dst_ref=dst, send_sem=send, recv_sem=recv,
        device_id=device, device_id_type=MESH,
    )


def kernel(
    a_hbm, l_hbm, mask_ref, dinv_hbm, off_ref, diag_ref,
    a_ref, l_ref, dinv_ref, masked, turned, a_in, a_high, a_low, m, p, c, yr, t, zb, cs, cx, cz, dg,
    fetch, s_a, r_a, s_first, s_right, s_left, s_x, r_m, s_c, r_c, s_y, r_y, s_z, r_z,
    s_cx, r_cx, s_cz, r_cz, s_dg, r_dg,
):
    row, col = lax.axis_index("prow"), lax.axis_index("pcol")
    x, zl = lax.div(row, ZL), lax.rem(row, ZL)
    zh, y, co = lax.div(col, 8), lax.rem(lax.div(col, 2), Y), lax.rem(col, 2)

    def device(x, zl, zh, y, co):
        return (x * ZL + zl, zh * 8 + y * 2 + co)

    kind = lax.rem(lax.div(x + 1, 2), 2)
    x_a, x_m = x + 1 - 2 * lax.rem(x, 2), 3 - x
    home = co == kind
    mine = lax.rem(lax.div(x, 2) + zh, 2)

    first_to = device(
        lax.rem(zl + lax.div(x, 2), 2) * 2 + lax.rem(lax.rem(zl + lax.div(x, 2), 2) + co, 2),
        2 * y + 1 - zh,
        lax.div(x, 2), 2 * lax.rem(x, 2) + lax.div(zl, 4), lax.rem(lax.div(zl, 2), 2),
    )
    first_slot = 2 * y + 1 - zh
    first_half = lax.rem(zl, 2)
    first_from = device(
        2 * zh + lax.div(y, 2),
        4 * lax.rem(y, 2) + 2 * co + mine,
        1 - lax.rem(zl, 2), lax.div(zl, 2), kind,
    )
    sibling = device(x, zl, zh, y, 1 - co)
    partner = device(x_m, zl, zh, y, co)
    a_partner = device(x_a, zl, zh, y, co)

    def x_peer(step):
        return device(lax.rem(x + step, X), zl, zh, y, co)

    def z_peer(step):
        return device(x, lax.rem(zl + step, ZL), zh, y, co)

    def y_peer(step):
        return device(x, zl, zh, lax.rem(y + step, Y), co)

    def end_peer(half):
        return device(jnp.where(home, x, x_a), zl, half, y, kind)

    fetch_l = pltpu.make_async_copy(l_hbm, l_ref, fetch.at[0])
    fetch_a = pltpu.make_async_copy(a_hbm, a_ref, fetch.at[1])
    fetch_dinv = pltpu.make_async_copy(dinv_hbm, dinv_ref, fetch.at[2])
    fetch_l.start()
    fetch_a.start()
    fetch_dinv.start()

    barrier = pltpu.get_barrier_semaphore()

    def greet(who):
        pl.semaphore_signal(barrier, inc=1, device_id=who, device_id_type=MESH)

    greet(first_from)
    greet(sibling)
    for step in range(1, X):
        greet(x_peer(step))
    for step in range(1, Y):
        greet(y_peer(step))
    for step in range(1, ZL):
        greet(z_peer(step))
    greet(end_peer(1 - zh))

    @pl.when(jnp.logical_not(home))
    def _():
        greet(end_peer(zh))

    fetch_l.wait()
    for block in range(3):
        rows = pl.ds(block * 128, 128)
        member = mask_ref[0, block].astype(jnp.float32)
        masked[rows, :] = l_ref[rows, :] * member

    pl.semaphore_wait(barrier, jnp.where(home, 16, 17))

    def spot(j, half, part):
        return m.at[j, half, pl.ds(part * (384 // PARTS), 384 // PARTS), :]

    def first(part):
        return copy_to(
            masked.at[pl.ds(part * (384 // PARTS), 384 // PARTS), :],
            spot(first_slot, first_half, part),
            s_first.at[part], r_m.at[first_slot, first_half, part], first_to,
        )

    for part in range(PARTS):
        first(part).start()

    def send_a(piece):
        rows = pl.ds(piece * 128, 128)
        return copy_to(
            a_ref.at[rows, :], a_in.at[rows, :], s_a.at[piece], r_a.at[piece], a_partner
        )

    fetch_a.wait()
    for piece in range(PIECES):
        send_a(piece).start()
    high, low = split(a_ref[...])
    a_high[kind], a_low[kind] = high, low
    high, low = split(masked[...].T)
    turned[0], turned[1] = high, low

    def order(i):
        half = lax.div(i + 1, 2)
        near = jnp.where(lax.rem(i, 2) == 1, zl - half, zl + half)
        far = jnp.where(zl <= 3, i, 7 - i)
        return jnp.where(i <= 2 * jnp.minimum(zl, 7 - zl), near, far)

    def to_right(j, part):
        here = spot(j, mine, part)
        return copy_to(
            here, here, s_right.at[j, part], r_m.at[j, mine, part],
            device(x, jnp.minimum(zl + 1, 7), zh, y, co),
        )

    def to_left(j, part):
        here = spot(j, mine, part)
        return copy_to(
            here, here, s_left.at[j, part], r_m.at[j, mine, part],
            device(x, jnp.maximum(zl - 1, 0), zh, y, co),
        )

    def to_partner(j, part):
        here = spot(j, mine, part)
        return copy_to(here, here, s_x.at[j, part], r_m.at[j, mine, part], partner)

    def arrival(j, half, part):
        here = spot(j, half, part)
        return copy_to(here, here, s_first.at[0], r_m.at[j, half, part], partner)

    def to_sibling(j):
        return copy_to(p.at[j, 1 - co], c.at[j], s_c.at[j], r_c.at[j], sibling)

    def to_owner(j):
        owner = lax.div(j, 2)
        slot = lax.rem(y - owner + Y, Y) - 1
        half = 1 - lax.rem(j, 2)
        return copy_to(
            p.at[j, co], yr.at[half, slot], s_y.at[j], r_y.at[half, slot],
            device(x, zl, zh, owner, co),
        )

    def to_end(half):
        return copy_to(t.at[half], zb.at[zh], s_z.at[half], r_z.at[zh], end_peer(half))

    def goes_right(j):
        return jnp.logical_and(j <= zl, zl < 7)

    def goes_left(j):
        return jnp.logical_and(j >= zl, zl > 0)

    def multiply(j, q):
        p[j, q] = product(a_high[q], a_low[q], m[j].reshape(768, 128))

    def step(i, carry):
        @pl.when(i < 8)
        def _():
            j = order(i)
            right, left = goes_right(j), goes_left(j)
            for part in range(PARTS):
                arrival(j, mine, part).wait_recv()

                @pl.when(right)
                def _(part=part):
                    to_right(j, part).start()

                @pl.when(left)
                def _(part=part):
                    to_left(j, part).start()

                to_partner(j, part).start()

        @pl.when(jnp.logical_and(i >= LEAD, i < LEAD + 8))
        def _():
            j = order(i - LEAD)
            for part in range(PARTS):
                arrival(j, 1 - mine, part).wait_recv()
            multiply(j, kind)

            @pl.when(jnp.logical_not(home))
            def _():
                to_sibling(j).start()

        @pl.when(i == LAG)
        def _():
            for piece in range(PIECES):
                send_a(piece).wait_recv()
            high, low = split(a_in[...])
            a_high[1 - kind], a_low[1 - kind] = high, low

        @pl.when(jnp.logical_and(i >= LAG, i < LAG + 8))
        def _():
            j = order(i - LAG)
            multiply(j, 1 - kind)

            @pl.when(home)
            def _():
                to_sibling(j).start()

        k = i - jnp.where(home, LEAD + 1, LAG + 1)

        @pl.when(jnp.logical_and(k >= 0, k < 8))
        def _():
            j = order(k)
            to_sibling(j).wait_recv()
            p[j, co] = p[j, co] + c[j]

            @pl.when(lax.div(j, 2) != y)
            def _():
                to_owner(j).start()

        @pl.when(jnp.logical_and(k >= TRAIL, k < TRAIL + 8))
        def _():
            j = order(k - TRAIL)
            half = 1 - lax.rem(j, 2)

            @pl.when(lax.div(j, 2) == y)
            def _():
                for slot in range(3):
                    copy_to(
                        t.at[0], yr.at[half, slot], s_y.at[0], r_y.at[half, slot], sibling
                    ).wait_recv()
                total = (p[j, co] + yr[half, 0]) + (yr[half, 1] + yr[half, 2])
                stays = jnp.logical_and(home, half == zh)

                @pl.when(stays)
                def _():
                    zb[zh] = total

                @pl.when(jnp.logical_not(stays))
                def _():
                    t[half] = total
                    to_end(half).start()

        return carry

    lax.fori_loop(0, 8 + LAG + 1 + TRAIL, step, 0)

    def end_arrival(half):
        return copy_to(t.at[0], zb.at[half], s_z.at[0], r_z.at[half], sibling)

    end_arrival(1 - zh).wait_recv()

    @pl.when(jnp.logical_not(home))
    def _():
        end_arrival(zh).wait_recv()

    for block in range(3):
        rows = pl.ds(block * 128, 128)
        member = mask_ref[0, block].astype(jnp.float32)
        off_ref[rows, :] = -((zb[0, rows, :] + zb[1, rows, :]) * member)

    correction = product(turned[0], turned[1], off_ref[...])
    for other in range(X):
        cs[other] = correction[other * 32 : other * 32 + 32, :]

    def corr_x(step):
        return copy_to(
            cs.at[lax.rem(x + step, X)], cx.at[step - 1], s_cx.at[step - 1], r_cx.at[step - 1],
            x_peer(step),
        )

    def corr_z(step):
        return copy_to(cz.at[zl], cz.at[zl], s_cz.at[step - 1], r_cz.at[zl], z_peer(step))

    def corr_back(step):
        return copy_to(dg.at[x], dg.at[x], s_dg.at[step - 1], r_dg.at[x], x_peer(step))

    for step_ in range(1, X):
        corr_x(step_).start()
    for step_ in range(1, X):
        corr_x(step_).wait_recv()
    cz[zl] = (cs[x] + cx[0]) + (cx[1] + cx[2])
    for step_ in range(1, ZL):
        corr_z(step_).start()
    for step_ in range(1, ZL):
        other = lax.rem(zl + step_, ZL)
        copy_to(cz.at[other], cz.at[other], s_cz.at[0], r_cz.at[other], sibling).wait_recv()
    dg[x] = ((cz[0] + cz[1]) + (cz[2] + cz[3])) + ((cz[4] + cz[5]) + (cz[6] + cz[7]))
    for step_ in range(1, X):
        corr_back(step_).start()
    for step_ in range(1, X):
        other = lax.rem(x + step_, X)
        copy_to(dg.at[other], dg.at[other], s_dg.at[0], r_dg.at[other], sibling).wait_recv()
    fetch_dinv.wait()
    for other in range(X):
        rows = pl.ds(other * 32, 32)
        diag_ref[0, rows, :] = dinv_ref[0, rows, :] - dg[other]

    for part in range(PARTS):
        first(part).wait_send()
    for piece in range(PIECES):
        send_a(piece).wait_send()

    def finish(j, carry):
        to_sibling(j).wait_send()
        for part in range(PARTS):
            to_partner(j, part).wait_send()

            @pl.when(goes_right(j))
            def _(part=part):
                to_right(j, part).wait_send()

            @pl.when(goes_left(j))
            def _(part=part):
                to_left(j, part).wait_send()

        @pl.when(lax.div(j, 2) != y)
        def _():
            to_owner(j).wait_send()

        return carry

    lax.fori_loop(0, 8, finish, 0)
    to_end(1 - zh).wait_send()

    @pl.when(jnp.logical_not(home))
    def _():
        to_end(zh).wait_send()

    for step_ in range(1, X):
        corr_x(step_).wait_send()
        corr_back(step_).wait_send()
    for step_ in range(1, ZL):
        corr_z(step_).wait_send()


def on_device(inverse_part, lower_panel, struct_mask, diag_inverse):
    f32, bf16 = jnp.float32, jnp.bfloat16
    dma = pltpu.SemaphoreType.DMA
    hbm = pl.BlockSpec(memory_space=pl.ANY)
    vmem = pl.BlockSpec(memory_space=pltpu.VMEM)
    return tuple(
        pl.pallas_call(
            kernel,
            out_shape=(
                jax.ShapeDtypeStruct((384, 128), f32),
                jax.ShapeDtypeStruct((1, 128, 128), f32),
            ),
            in_specs=[hbm, hbm, pl.BlockSpec(memory_space=pltpu.SMEM), hbm],
            out_specs=(vmem, vmem),
            scratch_shapes=[
                pltpu.VMEM((384, 768), f32),
                pltpu.VMEM((384, 128), f32),
                pltpu.VMEM((1, 128, 128), f32),
                pltpu.VMEM((384, 128), f32),
                pltpu.VMEM((2, 128, 384), bf16),
                pltpu.VMEM((384, 768), f32),
                pltpu.VMEM((2, 384, 768), bf16),
                pltpu.VMEM((2, 384, 768), bf16),
                pltpu.VMEM((8, 2, 384, 128), f32),
                pltpu.VMEM((8, 2, 384, 128), f32),
                pltpu.VMEM((8, 384, 128), f32),
                pltpu.VMEM((2, 3, 384, 128), f32),
                pltpu.VMEM((2, 384, 128), f32),
                pltpu.VMEM((2, 384, 128), f32),
                pltpu.VMEM((4, 32, 128), f32),
                pltpu.VMEM((3, 32, 128), f32),
                pltpu.VMEM((8, 32, 128), f32),
                pltpu.VMEM((4, 32, 128), f32),
                dma((3,)), dma((PIECES,)), dma((PIECES,)), dma((PARTS,)),
                dma((8, PARTS)), dma((8, PARTS)), dma((8, PARTS)), dma((8, 2, PARTS)),
                dma((8,)), dma((8,)), dma((8,)), dma((2, 3)), dma((2,)), dma((2,)),
                dma((3,)), dma((3,)), dma((7,)), dma((8,)), dma((3,)), dma((4,)),
            ],
            compiler_params=pltpu.CompilerParams(
                collective_id=0, has_side_effects=True, vmem_limit_bytes=63 * 1024 * 1024
            ),
            cost_estimate=pl.CostEstimate(
                flops=2 * 3 * 384 * 768 * 2048, bytes_accessed=4_000_000, transcendentals=0
            ),
        )(inverse_part, lower_panel, struct_mask, diag_inverse)
    )


def solution(mesh):
    return jax.shard_map(
        on_device,
        mesh=mesh,
        in_specs=(P("prow", "pcol"), P("prow", "pcol"), P("pcol", "prow"), P("pcol", None, None)),
        out_specs=(P("prow", "pcol"), P("pcol", None, None)),
        check_vma=False,
    )
```

```python
import jax
import jax.numpy as jnp
from jax import lax
from jax.experimental import pallas as pl
from jax.experimental.pallas import tpu as pltpu
from jax.sharding import PartitionSpec as P

MESH = pl.DeviceIdType.MESH
X, ZL, ZH, Y = 4, 8, 2, 4
PIECES = 3
PARTS = 3
LAG = 4
LEAD = 2
PASS = 2
TRAIL = 4


def split(value):
    high = value.astype(jnp.bfloat16)
    return high, (value - high.astype(jnp.float32)).astype(jnp.bfloat16)


def product(left_high, left_low, right):
    high, low = split(right)
    width = right.shape[1]
    both = jnp.dot(
        left_high, jnp.concatenate([high, low], axis=1), preferred_element_type=jnp.float32
    )
    rest = jnp.dot(left_low, high, preferred_element_type=jnp.float32)
    return both[:, :width] + (both[:, width:] + rest)


def copy_to(src, dst, send, recv, device):
    return pltpu.make_async_remote_copy(
        src_ref=src, dst_ref=dst, send_sem=send, recv_sem=recv,
        device_id=device, device_id_type=MESH,
    )


def kernel(
    a_hbm, l_hbm, mask_ref, dinv_hbm, off_ref, diag_ref,
    a_ref, l_ref, dinv_ref, masked, turned, a_in, a_high, a_low, m, p, c, far, yr, t, zb, cs, cx, cz, dg,
    fetch, s_a, r_a, s_first, s_right, s_left, s_x, r_m, s_c, r_c, s_y, r_y, r_far, s_z, r_z,
    s_cx, r_cx, s_cz, r_cz, s_dg, r_dg,
):
    row, col = lax.axis_index("prow"), lax.axis_index("pcol")
    x, zl = lax.div(row, ZL), lax.rem(row, ZL)
    zh, y, co = lax.div(col, 8), lax.rem(lax.div(col, 2), Y), lax.rem(col, 2)

    def device(x, zl, zh, y, co):
        return (x * ZL + zl, zh * 8 + y * 2 + co)

    kind = lax.rem(lax.div(x + 1, 2), 2)
    x_a, x_m = x + 1 - 2 * lax.rem(x, 2), 3 - x
    home = co == kind
    mine = lax.rem(lax.div(x, 2) + zh, 2)

    first_to = device(
        lax.rem(zl + lax.div(x, 2), 2) * 2 + lax.rem(lax.rem(zl + lax.div(x, 2), 2) + co, 2),
        2 * y + 1 - zh,
        lax.div(x, 2), 2 * lax.rem(x, 2) + lax.div(zl, 4), lax.rem(lax.div(zl, 2), 2),
    )
    first_slot = 2 * y + 1 - zh
    first_half = lax.rem(zl, 2)
    first_from = device(
        2 * zh + lax.div(y, 2),
        4 * lax.rem(y, 2) + 2 * co + mine,
        1 - lax.rem(zl, 2), lax.div(zl, 2), kind,
    )
    sibling = device(x, zl, zh, y, 1 - co)
    partner = device(x_m, zl, zh, y, co)
    a_partner = device(x_a, zl, zh, y, co)

    def x_peer(step):
        return device(lax.rem(x + step, X), zl, zh, y, co)

    def z_peer(step):
        return device(x, lax.rem(zl + step, ZL), zh, y, co)

    def y_peer(step):
        return device(x, zl, zh, lax.rem(y + step, Y), co)

    def end_peer(half):
        return device(jnp.where(home, x, x_a), zl, half, y, kind)

    fetch_l = pltpu.make_async_copy(l_hbm, l_ref, fetch.at[0])
    fetch_a = pltpu.make_async_copy(a_hbm, a_ref, fetch.at[1])
    fetch_dinv = pltpu.make_async_copy(dinv_hbm, dinv_ref, fetch.at[2])
    fetch_l.start()
    fetch_a.start()
    fetch_dinv.start()

    barrier = pltpu.get_barrier_semaphore()

    def greet(who):
        pl.semaphore_signal(barrier, inc=1, device_id=who, device_id_type=MESH)

    greet(first_from)
    greet(sibling)
    for step in range(1, X):
        greet(x_peer(step))
    for step in range(1, Y):
        greet(y_peer(step))
    for step in range(1, ZL):
        greet(z_peer(step))
    greet(end_peer(1 - zh))

    @pl.when(jnp.logical_not(home))
    def _():
        greet(end_peer(zh))

    fetch_l.wait()
    for block in range(3):
        rows = pl.ds(block * 128, 128)
        member = mask_ref[0, block].astype(jnp.float32)
        masked[rows, :] = l_ref[rows, :] * member

    pl.semaphore_wait(barrier, jnp.where(home, 16, 17))

    def spot(j, half, part):
        return m.at[j, half, pl.ds(part * (384 // PARTS), 384 // PARTS), :]

    def first(part):
        return copy_to(
            masked.at[pl.ds(part * (384 // PARTS), 384 // PARTS), :],
            spot(first_slot, first_half, part),
            s_first.at[part], r_m.at[first_slot, first_half, part], first_to,
        )

    for part in range(PARTS):
        first(part).start()

    def send_a(piece):
        rows = pl.ds(piece * 128, 128)
        return copy_to(
            a_ref.at[rows, :], a_in.at[rows, :], s_a.at[piece], r_a.at[piece], a_partner
        )

    fetch_a.wait()
    for piece in range(PIECES):
        send_a(piece).start()
    high, low = split(a_ref[...])
    a_high[kind], a_low[kind] = high, low
    high, low = split(masked[...].T)
    turned[0], turned[1] = high, low

    def order(i):
        half = lax.div(i + 1, 2)
        near = jnp.where(lax.rem(i, 2) == 1, zl - half, zl + half)
        far = jnp.where(zl <= 3, i, 7 - i)
        return jnp.where(i <= 2 * jnp.minimum(zl, 7 - zl), near, far)

    def to_right(j, part):
        here = spot(j, mine, part)
        return copy_to(
            here, here, s_right.at[j, part], r_m.at[j, mine, part],
            device(x, jnp.minimum(zl + 1, 7), zh, y, co),
        )

    def to_left(j, part):
        here = spot(j, mine, part)
        return copy_to(
            here, here, s_left.at[j, part], r_m.at[j, mine, part],
            device(x, jnp.maximum(zl - 1, 0), zh, y, co),
        )

    def to_partner(j, part):
        here = spot(j, mine, part)
        return copy_to(here, here, s_x.at[j, part], r_m.at[j, mine, part], partner)

    def arrival(j, half, part):
        here = spot(j, half, part)
        return copy_to(here, here, s_first.at[0], r_m.at[j, half, part], partner)

    def to_sibling(j):
        return copy_to(p.at[j, 1 - co], c.at[j], s_c.at[j], r_c.at[j], sibling)

    def role(j):
        half = 1 - lax.rem(j, 2)
        toward = 1 - 2 * half
        return lax.rem(y - lax.div(j, 2) + Y, Y), half, toward

    def to_owner(j):
        _, half, toward = role(j)
        owner = lax.div(j, 2)
        side = jnp.where(lax.rem(y - owner + Y, Y) == 1, 0, 1)
        return copy_to(
            p.at[j, co], yr.at[half, side], s_y.at[j], r_y.at[half, side],
            device(x, zl, zh, owner, co),
        )

    def to_between(j):
        _, half, toward = role(j)
        return copy_to(
            p.at[j, co], far.at[half], s_y.at[j], r_far.at[half],
            device(x, zl, zh, lax.rem(y - toward + Y, Y), co),
        )

    def to_end(half):
        return copy_to(t.at[half], zb.at[zh], s_z.at[half], r_z.at[zh], end_peer(half))

    def goes_right(j):
        return jnp.logical_and(j <= zl, zl < 7)

    def goes_left(j):
        return jnp.logical_and(j >= zl, zl > 0)

    def multiply(j, q):
        p[j, q] = product(a_high[q], a_low[q], m[j].reshape(768, 128))

    def step(i, carry):
        @pl.when(i < 8)
        def _():
            j = order(i)
            right, left = goes_right(j), goes_left(j)
            for part in range(PARTS):
                arrival(j, mine, part).wait_recv()

                @pl.when(right)
                def _(part=part):
                    to_right(j, part).start()

                @pl.when(left)
                def _(part=part):
                    to_left(j, part).start()

                to_partner(j, part).start()

        @pl.when(jnp.logical_and(i >= LEAD, i < LEAD + 8))
        def _():
            j = order(i - LEAD)
            for part in range(PARTS):
                arrival(j, 1 - mine, part).wait_recv()
            multiply(j, kind)

            @pl.when(jnp.logical_not(home))
            def _():
                to_sibling(j).start()

        @pl.when(i == LAG)
        def _():
            for piece in range(PIECES):
                send_a(piece).wait_recv()
            high, low = split(a_in[...])
            a_high[1 - kind], a_low[1 - kind] = high, low

        @pl.when(jnp.logical_and(i >= LAG, i < LAG + 8))
        def _():
            j = order(i - LAG)
            multiply(j, 1 - kind)

            @pl.when(home)
            def _():
                to_sibling(j).start()

        k = i - jnp.where(home, LEAD + 1, LAG + 1)

        @pl.when(jnp.logical_and(k >= 0, k < 8))
        def _():
            j = order(k)
            to_sibling(j).wait_recv()
            p[j, co] = p[j, co] + c[j]

            distance, _, toward = role(j)

            @pl.when(distance == lax.rem(Y - toward, Y))
            def _():
                to_owner(j).start()

            @pl.when(distance == 2)
            def _():
                to_between(j).start()

        @pl.when(jnp.logical_and(k >= PASS, k < PASS + 8))
        def _():
            j = order(k - PASS)
            distance, half, toward = role(j)

            @pl.when(distance == lax.rem(Y + toward, Y))
            def _():
                copy_to(t.at[0], far.at[half], s_y.at[0], r_far.at[half], sibling).wait_recv()
                p[j, co] = p[j, co] + far[half]
                to_owner(j).start()

        @pl.when(jnp.logical_and(k >= TRAIL, k < TRAIL + 8))
        def _():
            j = order(k - TRAIL)
            half = 1 - lax.rem(j, 2)

            @pl.when(lax.div(j, 2) == y)
            def _():
                for slot in range(2):
                    copy_to(
                        t.at[0], yr.at[half, slot], s_y.at[0], r_y.at[half, slot], sibling
                    ).wait_recv()
                total = p[j, co] + (yr[half, 0] + yr[half, 1])
                stays = jnp.logical_and(home, half == zh)

                @pl.when(stays)
                def _():
                    zb[zh] = total

                @pl.when(jnp.logical_not(stays))
                def _():
                    t[half] = total
                    to_end(half).start()

        return carry

    lax.fori_loop(0, 8 + LAG + 1 + TRAIL, step, 0)

    def end_arrival(half):
        return copy_to(t.at[0], zb.at[half], s_z.at[0], r_z.at[half], sibling)

    end_arrival(1 - zh).wait_recv()

    @pl.when(jnp.logical_not(home))
    def _():
        end_arrival(zh).wait_recv()

    for block in range(3):
        rows = pl.ds(block * 128, 128)
        member = mask_ref[0, block].astype(jnp.float32)
        off_ref[rows, :] = -((zb[0, rows, :] + zb[1, rows, :]) * member)

    correction = product(turned[0], turned[1], off_ref[...])
    for other in range(X):
        cs[other] = correction[other * 32 : other * 32 + 32, :]

    def corr_x(step):
        return copy_to(
            cs.at[lax.rem(x + step, X)], cx.at[step - 1], s_cx.at[step - 1], r_cx.at[step - 1],
            x_peer(step),
        )

    def corr_z(step):
        return copy_to(cz.at[zl], cz.at[zl], s_cz.at[step - 1], r_cz.at[zl], z_peer(step))

    def corr_back(step):
        return copy_to(dg.at[x], dg.at[x], s_dg.at[step - 1], r_dg.at[x], x_peer(step))

    for step_ in range(1, X):
        corr_x(step_).start()
    for step_ in range(1, X):
        corr_x(step_).wait_recv()
    cz[zl] = (cs[x] + cx[0]) + (cx[1] + cx[2])
    for step_ in range(1, ZL):
        corr_z(step_).start()
    for step_ in range(1, ZL):
        other = lax.rem(zl + step_, ZL)
        copy_to(cz.at[other], cz.at[other], s_cz.at[0], r_cz.at[other], sibling).wait_recv()
    dg[x] = ((cz[0] + cz[1]) + (cz[2] + cz[3])) + ((cz[4] + cz[5]) + (cz[6] + cz[7]))
    for step_ in range(1, X):
        corr_back(step_).start()
    for step_ in range(1, X):
        other = lax.rem(x + step_, X)
        copy_to(dg.at[other], dg.at[other], s_dg.at[0], r_dg.at[other], sibling).wait_recv()
    fetch_dinv.wait()
    for other in range(X):
        rows = pl.ds(other * 32, 32)
        diag_ref[0, rows, :] = dinv_ref[0, rows, :] - dg[other]

    for part in range(PARTS):
        first(part).wait_send()
    for piece in range(PIECES):
        send_a(piece).wait_send()

    def finish(j, carry):
        to_sibling(j).wait_send()
        for part in range(PARTS):
            to_partner(j, part).wait_send()

            @pl.when(goes_right(j))
            def _(part=part):
                to_right(j, part).wait_send()

            @pl.when(goes_left(j))
            def _(part=part):
                to_left(j, part).wait_send()

        distance, _, _ = role(j)

        @pl.when(distance == 2)
        def _():
            to_between(j).wait_send()

        @pl.when(lax.rem(distance, 2) == 1)
        def _():
            to_owner(j).wait_send()

        return carry

    lax.fori_loop(0, 8, finish, 0)
    to_end(1 - zh).wait_send()

    @pl.when(jnp.logical_not(home))
    def _():
        to_end(zh).wait_send()

    for step_ in range(1, X):
        corr_x(step_).wait_send()
        corr_back(step_).wait_send()
    for step_ in range(1, ZL):
        corr_z(step_).wait_send()


def on_device(inverse_part, lower_panel, struct_mask, diag_inverse):
    f32, bf16 = jnp.float32, jnp.bfloat16
    dma = pltpu.SemaphoreType.DMA
    hbm = pl.BlockSpec(memory_space=pl.ANY)
    vmem = pl.BlockSpec(memory_space=pltpu.VMEM)
    return tuple(
        pl.pallas_call(
            kernel,
            out_shape=(
                jax.ShapeDtypeStruct((384, 128), f32),
                jax.ShapeDtypeStruct((1, 128, 128), f32),
            ),
            in_specs=[hbm, hbm, pl.BlockSpec(memory_space=pltpu.SMEM), hbm],
            out_specs=(vmem, vmem),
            scratch_shapes=[
                pltpu.VMEM((384, 768), f32),
                pltpu.VMEM((384, 128), f32),
                pltpu.VMEM((1, 128, 128), f32),
                pltpu.VMEM((384, 128), f32),
                pltpu.VMEM((2, 128, 384), bf16),
                pltpu.VMEM((384, 768), f32),
                pltpu.VMEM((2, 384, 768), bf16),
                pltpu.VMEM((2, 384, 768), bf16),
                pltpu.VMEM((8, 2, 384, 128), f32),
                pltpu.VMEM((8, 2, 384, 128), f32),
                pltpu.VMEM((8, 384, 128), f32),
                pltpu.VMEM((2, 384, 128), f32),
                pltpu.VMEM((2, 2, 384, 128), f32),
                pltpu.VMEM((2, 384, 128), f32),
                pltpu.VMEM((2, 384, 128), f32),
                pltpu.VMEM((4, 32, 128), f32),
                pltpu.VMEM((3, 32, 128), f32),
                pltpu.VMEM((8, 32, 128), f32),
                pltpu.VMEM((4, 32, 128), f32),
                dma((3,)), dma((PIECES,)), dma((PIECES,)), dma((PARTS,)),
                dma((8, PARTS)), dma((8, PARTS)), dma((8, PARTS)), dma((8, 2, PARTS)),
                dma((8,)), dma((8,)), dma((8,)), dma((2, 2)), dma((2,)), dma((2,)), dma((2,)),
                dma((3,)), dma((3,)), dma((7,)), dma((8,)), dma((3,)), dma((4,)),
            ],
            compiler_params=pltpu.CompilerParams(
                collective_id=0, has_side_effects=True, vmem_limit_bytes=63 * 1024 * 1024
            ),
            cost_estimate=pl.CostEstimate(
                flops=2 * 3 * 384 * 768 * 2048, bytes_accessed=4_000_000, transcendentals=0
            ),
        )(inverse_part, lower_panel, struct_mask, diag_inverse)
    )


def solution(mesh):
    return jax.shard_map(
        on_device,
        mesh=mesh,
        in_specs=(P("prow", "pcol"), P("prow", "pcol"), P("pcol", "prow"), P("pcol", None, None)),
        out_specs=(P("prow", "pcol"), P("pcol", None, None)),
        check_vma=False,
    )
```

```python
import jax
import jax.numpy as jnp
from jax import lax
from jax.experimental import pallas as pl
from jax.experimental.pallas import tpu as pltpu
from jax.sharding import PartitionSpec as P

MESH = pl.DeviceIdType.MESH
X, ZL, ZH, Y = 4, 8, 2, 4
PIECES = 3
PARTS = 3
LAG = 3
PASS = 2
TRAIL = 4


def split(value):
    high = value.astype(jnp.bfloat16)
    return high, (value - high.astype(jnp.float32)).astype(jnp.bfloat16)


def product(left_high, left_low, right):
    high, low = split(right)
    width = right.shape[1]
    both = jnp.dot(
        left_high, jnp.concatenate([high, low], axis=1), preferred_element_type=jnp.float32
    )
    rest = jnp.dot(left_low, high, preferred_element_type=jnp.float32)
    return both[:, :width] + (both[:, width:] + rest)


def copy_to(src, dst, send, recv, device):
    return pltpu.make_async_remote_copy(
        src_ref=src, dst_ref=dst, send_sem=send, recv_sem=recv,
        device_id=device, device_id_type=MESH,
    )


def kernel(
    a_hbm, l_hbm, mask_ref, dinv_hbm, off_ref, diag_ref,
    a_ref, l_ref, dinv_ref, masked, turned, a_in, a_high, a_low, m, p, c, far, yr, t, zb, cs, cx, cz, dg,
    fetch, s_a, r_a, s_first, s_right, s_left, s_x, r_m, s_c, r_c, s_y, r_y, r_far, s_z, r_z,
    s_cx, r_cx, s_cz, r_cz, s_dg, r_dg,
):
    row, col = lax.axis_index("prow"), lax.axis_index("pcol")
    x, zl = lax.div(row, ZL), lax.rem(row, ZL)
    zh, y, co = lax.div(col, 8), lax.rem(lax.div(col, 2), Y), lax.rem(col, 2)

    def device(x, zl, zh, y, co):
        return (x * ZL + zl, zh * 8 + y * 2 + co)

    kind = lax.rem(lax.div(x + 1, 2), 2)
    x_a, x_m = x + 1 - 2 * lax.rem(x, 2), 3 - x
    home = co == kind
    mine = lax.rem(lax.div(x, 2) + zh, 2)

    first_to = device(
        lax.rem(zl + lax.div(x, 2), 2) * 2 + lax.rem(lax.rem(zl + lax.div(x, 2), 2) + co, 2),
        2 * y + 1 - zh,
        lax.div(x, 2), 2 * lax.rem(x, 2) + lax.div(zl, 4), lax.rem(lax.div(zl, 2), 2),
    )
    first_slot = 2 * y + 1 - zh
    first_half = lax.rem(zl, 2)
    first_from = device(
        2 * zh + lax.div(y, 2),
        4 * lax.rem(y, 2) + 2 * co + mine,
        1 - lax.rem(zl, 2), lax.div(zl, 2), kind,
    )
    sibling = device(x, zl, zh, y, 1 - co)
    partner = device(x_m, zl, zh, y, co)
    a_partner = device(x_a, zl, zh, y, co)

    def x_peer(step):
        return device(lax.rem(x + step, X), zl, zh, y, co)

    def z_peer(step):
        return device(x, lax.rem(zl + step, ZL), zh, y, co)

    def y_peer(step):
        return device(x, zl, zh, lax.rem(y + step, Y), co)

    def end_peer(half):
        return device(jnp.where(home, x, x_a), zl, half, y, kind)

    fetch_l = pltpu.make_async_copy(l_hbm, l_ref, fetch.at[0])
    fetch_a = pltpu.make_async_copy(a_hbm, a_ref, fetch.at[1])
    fetch_dinv = pltpu.make_async_copy(dinv_hbm, dinv_ref, fetch.at[2])
    fetch_l.start()
    fetch_a.start()
    fetch_dinv.start()

    barrier = pltpu.get_barrier_semaphore()

    def greet(who):
        pl.semaphore_signal(barrier, inc=1, device_id=who, device_id_type=MESH)

    greet(first_from)
    greet(sibling)
    for step in range(1, X):
        greet(x_peer(step))
    for step in range(1, Y):
        greet(y_peer(step))
    for step in range(1, ZL):
        greet(z_peer(step))
    greet(end_peer(1 - zh))

    @pl.when(jnp.logical_not(home))
    def _():
        greet(end_peer(zh))

    fetch_l.wait()
    for block in range(3):
        rows = pl.ds(block * 128, 128)
        member = mask_ref[0, block].astype(jnp.float32)
        masked[rows, :] = l_ref[rows, :] * member

    pl.semaphore_wait(barrier, jnp.where(home, 16, 17))

    def spot(j, half, part):
        return m.at[j, half, pl.ds(part * (384 // PARTS), 384 // PARTS), :]

    def first(part):
        return copy_to(
            masked.at[pl.ds(part * (384 // PARTS), 384 // PARTS), :],
            spot(first_slot, first_half, part),
            s_first.at[part], r_m.at[first_slot, first_half, part], first_to,
        )

    for part in range(PARTS):
        first(part).start()

    def send_a(piece):
        rows = pl.ds(piece * 128, 128)
        return copy_to(
            a_ref.at[rows, :], a_in.at[rows, :], s_a.at[piece], r_a.at[piece], a_partner
        )

    fetch_a.wait()
    for piece in range(PIECES):
        send_a(piece).start()
    high, low = split(a_ref[...])
    a_high[kind], a_low[kind] = high, low
    high, low = split(masked[...].T)
    turned[0], turned[1] = high, low

    def order(i):
        half = lax.div(i + 1, 2)
        near = jnp.where(lax.rem(i, 2) == 1, zl - half, zl + half)
        far = jnp.where(zl <= 3, i, 7 - i)
        return jnp.where(i <= 2 * jnp.minimum(zl, 7 - zl), near, far)

    def to_right(j, part):
        here = spot(j, mine, part)
        return copy_to(
            here, here, s_right.at[j, part], r_m.at[j, mine, part],
            device(x, jnp.minimum(zl + 1, 7), zh, y, co),
        )

    def to_left(j, part):
        here = spot(j, mine, part)
        return copy_to(
            here, here, s_left.at[j, part], r_m.at[j, mine, part],
            device(x, jnp.maximum(zl - 1, 0), zh, y, co),
        )

    def to_partner(j, part):
        here = spot(j, mine, part)
        return copy_to(here, here, s_x.at[j, part], r_m.at[j, mine, part], partner)

    def arrival(j, half, part):
        here = spot(j, half, part)
        return copy_to(here, here, s_first.at[0], r_m.at[j, half, part], partner)

    def to_sibling(j):
        return copy_to(p.at[j, 1 - co], c.at[j], s_c.at[j], r_c.at[j], sibling)

    def role(j):
        half = 1 - lax.rem(j, 2)
        toward = 1 - 2 * half
        return lax.rem(y - lax.div(j, 2) + Y, Y), half, toward

    def to_owner(j):
        _, half, toward = role(j)
        owner = lax.div(j, 2)
        side = jnp.where(lax.rem(y - owner + Y, Y) == 1, 0, 1)
        return copy_to(
            p.at[j, co], yr.at[half, side], s_y.at[j], r_y.at[half, side],
            device(x, zl, zh, owner, co),
        )

    def to_between(j):
        _, half, toward = role(j)
        return copy_to(
            p.at[j, co], far.at[half], s_y.at[j], r_far.at[half],
            device(x, zl, zh, lax.rem(y - toward + Y, Y), co),
        )

    def to_end(half):
        return copy_to(t.at[half], zb.at[zh], s_z.at[half], r_z.at[zh], end_peer(half))

    def goes_right(j):
        return jnp.logical_and(j <= zl, zl < 7)

    def goes_left(j):
        return jnp.logical_and(j >= zl, zl > 0)

    def step(i, carry):
        @pl.when(i < 8)
        def _():
            j = order(i)
            right, left = goes_right(j), goes_left(j)
            for part in range(PARTS):
                arrival(j, mine, part).wait_recv()

                @pl.when(right)
                def _(part=part):
                    to_right(j, part).start()

                @pl.when(left)
                def _(part=part):
                    to_left(j, part).start()

                to_partner(j, part).start()

        @pl.when(i == LAG)
        def _():
            for piece in range(PIECES):
                send_a(piece).wait_recv()
            high, low = split(a_in[...])
            a_high[1 - kind], a_low[1 - kind] = high, low

        @pl.when(jnp.logical_and(i >= LAG, i < LAG + 8))
        def _():
            j = order(i - LAG)
            for part in range(PARTS):
                arrival(j, 1 - mine, part).wait_recv()
            p[j] = product(
                a_high[...].reshape(768, 768), a_low[...].reshape(768, 768), m[j].reshape(768, 128)
            ).reshape(2, 384, 128)
            to_sibling(j).start()

        k = i - (LAG + 1)

        @pl.when(jnp.logical_and(k >= 0, k < 8))
        def _():
            j = order(k)
            to_sibling(j).wait_recv()
            p[j, co] = p[j, co] + c[j]

            distance, _, toward = role(j)

            @pl.when(distance == lax.rem(Y - toward, Y))
            def _():
                to_owner(j).start()

            @pl.when(distance == 2)
            def _():
                to_between(j).start()

        @pl.when(jnp.logical_and(k >= PASS, k < PASS + 8))
        def _():
            j = order(k - PASS)
            distance, half, toward = role(j)

            @pl.when(distance == lax.rem(Y + toward, Y))
            def _():
                copy_to(t.at[0], far.at[half], s_y.at[0], r_far.at[half], sibling).wait_recv()
                p[j, co] = p[j, co] + far[half]
                to_owner(j).start()

        @pl.when(jnp.logical_and(k >= TRAIL, k < TRAIL + 8))
        def _():
            j = order(k - TRAIL)
            half = 1 - lax.rem(j, 2)

            @pl.when(lax.div(j, 2) == y)
            def _():
                for slot in range(2):
                    copy_to(
                        t.at[0], yr.at[half, slot], s_y.at[0], r_y.at[half, slot], sibling
                    ).wait_recv()
                total = p[j, co] + (yr[half, 0] + yr[half, 1])
                stays = jnp.logical_and(home, half == zh)

                @pl.when(stays)
                def _():
                    zb[zh] = total

                @pl.when(jnp.logical_not(stays))
                def _():
                    t[half] = total
                    to_end(half).start()

        return carry

    lax.fori_loop(0, 8 + LAG + 1 + TRAIL, step, 0)

    def end_arrival(half):
        return copy_to(t.at[0], zb.at[half], s_z.at[0], r_z.at[half], sibling)

    end_arrival(1 - zh).wait_recv()

    @pl.when(jnp.logical_not(home))
    def _():
        end_arrival(zh).wait_recv()

    for block in range(3):
        rows = pl.ds(block * 128, 128)
        member = mask_ref[0, block].astype(jnp.float32)
        off_ref[rows, :] = -((zb[0, rows, :] + zb[1, rows, :]) * member)

    correction = product(turned[0], turned[1], off_ref[...])
    for other in range(X):
        cs[other] = correction[other * 32 : other * 32 + 32, :]

    def corr_x(step):
        return copy_to(
            cs.at[lax.rem(x + step, X)], cx.at[step - 1], s_cx.at[step - 1], r_cx.at[step - 1],
            x_peer(step),
        )

    def corr_z(step):
        return copy_to(cz.at[zl], cz.at[zl], s_cz.at[step - 1], r_cz.at[zl], z_peer(step))

    def corr_back(step):
        return copy_to(dg.at[x], dg.at[x], s_dg.at[step - 1], r_dg.at[x], x_peer(step))

    for step_ in range(1, X):
        corr_x(step_).start()
    for step_ in range(1, X):
        corr_x(step_).wait_recv()
    cz[zl] = (cs[x] + cx[0]) + (cx[1] + cx[2])
    for step_ in range(1, ZL):
        corr_z(step_).start()
    for step_ in range(1, ZL):
        other = lax.rem(zl + step_, ZL)
        copy_to(cz.at[other], cz.at[other], s_cz.at[0], r_cz.at[other], sibling).wait_recv()
    dg[x] = ((cz[0] + cz[1]) + (cz[2] + cz[3])) + ((cz[4] + cz[5]) + (cz[6] + cz[7]))
    for step_ in range(1, X):
        corr_back(step_).start()
    for step_ in range(1, X):
        other = lax.rem(x + step_, X)
        copy_to(dg.at[other], dg.at[other], s_dg.at[0], r_dg.at[other], sibling).wait_recv()
    fetch_dinv.wait()
    for other in range(X):
        rows = pl.ds(other * 32, 32)
        diag_ref[0, rows, :] = dinv_ref[0, rows, :] - dg[other]

    for part in range(PARTS):
        first(part).wait_send()
    for piece in range(PIECES):
        send_a(piece).wait_send()

    def finish(j, carry):
        to_sibling(j).wait_send()
        for part in range(PARTS):
            to_partner(j, part).wait_send()

            @pl.when(goes_right(j))
            def _(part=part):
                to_right(j, part).wait_send()

            @pl.when(goes_left(j))
            def _(part=part):
                to_left(j, part).wait_send()

        distance, _, _ = role(j)

        @pl.when(distance == 2)
        def _():
            to_between(j).wait_send()

        @pl.when(lax.rem(distance, 2) == 1)
        def _():
            to_owner(j).wait_send()

        return carry

    lax.fori_loop(0, 8, finish, 0)
    to_end(1 - zh).wait_send()

    @pl.when(jnp.logical_not(home))
    def _():
        to_end(zh).wait_send()

    for step_ in range(1, X):
        corr_x(step_).wait_send()
        corr_back(step_).wait_send()
    for step_ in range(1, ZL):
        corr_z(step_).wait_send()


def on_device(inverse_part, lower_panel, struct_mask, diag_inverse):
    f32, bf16 = jnp.float32, jnp.bfloat16
    dma = pltpu.SemaphoreType.DMA
    hbm = pl.BlockSpec(memory_space=pl.ANY)
    vmem = pl.BlockSpec(memory_space=pltpu.VMEM)
    return tuple(
        pl.pallas_call(
            kernel,
            out_shape=(
                jax.ShapeDtypeStruct((384, 128), f32),
                jax.ShapeDtypeStruct((1, 128, 128), f32),
            ),
            in_specs=[hbm, hbm, pl.BlockSpec(memory_space=pltpu.SMEM), hbm],
            out_specs=(vmem, vmem),
            scratch_shapes=[
                pltpu.VMEM((384, 768), f32),
                pltpu.VMEM((384, 128), f32),
                pltpu.VMEM((1, 128, 128), f32),
                pltpu.VMEM((384, 128), f32),
                pltpu.VMEM((2, 128, 384), bf16),
                pltpu.VMEM((384, 768), f32),
                pltpu.VMEM((2, 384, 768), bf16),
                pltpu.VMEM((2, 384, 768), bf16),
                pltpu.VMEM((8, 2, 384, 128), f32),
                pltpu.VMEM((8, 2, 384, 128), f32),
                pltpu.VMEM((8, 384, 128), f32),
                pltpu.VMEM((2, 384, 128), f32),
                pltpu.VMEM((2, 2, 384, 128), f32),
                pltpu.VMEM((2, 384, 128), f32),
                pltpu.VMEM((2, 384, 128), f32),
                pltpu.VMEM((4, 32, 128), f32),
                pltpu.VMEM((3, 32, 128), f32),
                pltpu.VMEM((8, 32, 128), f32),
                pltpu.VMEM((4, 32, 128), f32),
                dma((3,)), dma((PIECES,)), dma((PIECES,)), dma((PARTS,)),
                dma((8, PARTS)), dma((8, PARTS)), dma((8, PARTS)), dma((8, 2, PARTS)),
                dma((8,)), dma((8,)), dma((8,)), dma((2, 2)), dma((2,)), dma((2,)), dma((2,)),
                dma((3,)), dma((3,)), dma((7,)), dma((8,)), dma((3,)), dma((4,)),
            ],
            compiler_params=pltpu.CompilerParams(
                collective_id=0, has_side_effects=True, vmem_limit_bytes=63 * 1024 * 1024
            ),
            cost_estimate=pl.CostEstimate(
                flops=2 * 3 * 384 * 768 * 2048, bytes_accessed=4_000_000, transcendentals=0
            ),
        )(inverse_part, lower_panel, struct_mask, diag_inverse)
    )


def solution(mesh):
    return jax.shard_map(
        on_device,
        mesh=mesh,
        in_specs=(P("prow", "pcol"), P("prow", "pcol"), P("pcol", "prow"), P("pcol", None, None)),
        out_specs=(P("prow", "pcol"), P("pcol", None, None)),
        check_vma=False,
    )
```

```python
import jax
import jax.numpy as jnp
from jax import lax
from jax.experimental import pallas as pl
from jax.experimental.pallas import tpu as pltpu
from jax.sharding import PartitionSpec as P

MESH = pl.DeviceIdType.MESH
X, ZL, ZH, Y = 4, 8, 2, 4
PIECES = 3
PARTS = 3
LAG = 3
ENDS = 3
PASS = 2
TRAIL = 4


def split(value):
    high = value.astype(jnp.bfloat16)
    return high, (value - high.astype(jnp.float32)).astype(jnp.bfloat16)


def product(left_high, left_low, right):
    high, low = split(right)
    width = right.shape[1]
    both = jnp.dot(
        left_high, jnp.concatenate([high, low], axis=1), preferred_element_type=jnp.float32
    )
    rest = jnp.dot(left_low, high, preferred_element_type=jnp.float32)
    return both[:, :width] + (both[:, width:] + rest)


def copy_to(src, dst, send, recv, device):
    return pltpu.make_async_remote_copy(
        src_ref=src, dst_ref=dst, send_sem=send, recv_sem=recv,
        device_id=device, device_id_type=MESH,
    )


def kernel(
    a_hbm, l_hbm, mask_ref, dinv_hbm, off_ref, diag_ref,
    a_ref, l_ref, dinv_ref, masked, turned, a_in, a_high, a_low, m, p, c, far, yr, t, rel, zb, cs, cx, cz, dg,
    fetch, s_a, r_a, s_first, s_right, s_left, s_x, r_m, s_c, r_c, s_y, r_y, r_far, s_rel, r_rel, s_on, s_z, r_z,
    s_cx, r_cx, s_cz, r_cz, s_dg, r_dg,
):
    row, col = lax.axis_index("prow"), lax.axis_index("pcol")
    x, zl = lax.div(row, ZL), lax.rem(row, ZL)
    zh, y, co = lax.div(col, 8), lax.rem(lax.div(col, 2), Y), lax.rem(col, 2)

    def device(x, zl, zh, y, co):
        return (x * ZL + zl, zh * 8 + y * 2 + co)

    kind = lax.rem(lax.div(x + 1, 2), 2)
    x_a, x_m = x + 1 - 2 * lax.rem(x, 2), 3 - x
    home = co == kind
    mine = lax.rem(lax.div(x, 2) + zh, 2)

    first_to = device(
        lax.rem(zl + lax.div(x, 2), 2) * 2 + lax.rem(lax.rem(zl + lax.div(x, 2), 2) + co, 2),
        2 * y + 1 - zh,
        lax.div(x, 2), 2 * lax.rem(x, 2) + lax.div(zl, 4), lax.rem(lax.div(zl, 2), 2),
    )
    first_slot = 2 * y + 1 - zh
    first_half = lax.rem(zl, 2)
    first_from = device(
        2 * zh + lax.div(y, 2),
        4 * lax.rem(y, 2) + 2 * co + mine,
        1 - lax.rem(zl, 2), lax.div(zl, 2), kind,
    )
    sibling = device(x, zl, zh, y, 1 - co)
    partner = device(x_m, zl, zh, y, co)
    a_partner = device(x_a, zl, zh, y, co)

    def x_peer(step):
        return device(lax.rem(x + step, X), zl, zh, y, co)

    def z_peer(step):
        return device(x, lax.rem(zl + step, ZL), zh, y, co)

    def y_peer(step):
        return device(x, zl, zh, lax.rem(y + step, Y), co)

    z = zh * ZL + zl
    way = jnp.where(home, 1, 15)
    x_end = jnp.where(home, x, x_a)

    def at_z(x, z, co):
        z = lax.rem(z, 16)
        return device(x, lax.rem(z, ZL), lax.div(z, ZL), y, co)

    relay = at_z(x, z + way, co)
    relayed = at_z(x, z + 16 - way, co)
    relayed_half = lax.div(lax.rem(z + 16 - way, 16), ZL)
    relay_end = at_z(x_end, z + 16 - way + 8, kind)
    relay_in = at_z(x_end, z + 8 + way, kind)
    direct = at_z(x_a, z, 1 - co)

    fetch_l = pltpu.make_async_copy(l_hbm, l_ref, fetch.at[0])
    fetch_a = pltpu.make_async_copy(a_hbm, a_ref, fetch.at[1])
    fetch_dinv = pltpu.make_async_copy(dinv_hbm, dinv_ref, fetch.at[2])
    fetch_l.start()
    fetch_a.start()
    fetch_dinv.start()

    barrier = pltpu.get_barrier_semaphore()

    def greet(who):
        pl.semaphore_signal(barrier, inc=1, device_id=who, device_id_type=MESH)

    greet(first_from)
    greet(sibling)
    for step in range(1, X):
        greet(x_peer(step))
    for step in range(1, Y):
        greet(y_peer(step))
    for step in range(1, ZL):
        greet(z_peer(step))
    greet(relayed)
    greet(relay_in)

    @pl.when(jnp.logical_not(home))
    def _():
        greet(direct)

    fetch_l.wait()
    for block in range(3):
        rows = pl.ds(block * 128, 128)
        member = mask_ref[0, block].astype(jnp.float32)
        masked[rows, :] = l_ref[rows, :] * member

    pl.semaphore_wait(barrier, jnp.where(home, 17, 18))

    def spot(j, half, part):
        return m.at[j, half, pl.ds(part * (384 // PARTS), 384 // PARTS), :]

    def first(part):
        return copy_to(
            masked.at[pl.ds(part * (384 // PARTS), 384 // PARTS), :],
            spot(first_slot, first_half, part),
            s_first.at[part], r_m.at[first_slot, first_half, part], first_to,
        )

    for part in range(PARTS):
        first(part).start()

    def send_a(piece):
        rows = pl.ds(piece * 128, 128)
        return copy_to(
            a_ref.at[rows, :], a_in.at[rows, :], s_a.at[piece], r_a.at[piece], a_partner
        )

    fetch_a.wait()
    for piece in range(PIECES):
        send_a(piece).start()
    high, low = split(a_ref[...])
    a_high[kind], a_low[kind] = high, low
    high, low = split(masked[...].T)
    turned[0], turned[1] = high, low

    def order(i):
        half = lax.div(i + 1, 2)
        near = jnp.where(lax.rem(i, 2) == 1, zl - half, zl + half)
        far = jnp.where(zl <= 3, i, 7 - i)
        return jnp.where(i <= 2 * jnp.minimum(zl, 7 - zl), near, far)

    def to_right(j, part):
        here = spot(j, mine, part)
        return copy_to(
            here, here, s_right.at[j, part], r_m.at[j, mine, part],
            device(x, jnp.minimum(zl + 1, 7), zh, y, co),
        )

    def to_left(j, part):
        here = spot(j, mine, part)
        return copy_to(
            here, here, s_left.at[j, part], r_m.at[j, mine, part],
            device(x, jnp.maximum(zl - 1, 0), zh, y, co),
        )

    def to_partner(j, part):
        here = spot(j, mine, part)
        return copy_to(here, here, s_x.at[j, part], r_m.at[j, mine, part], partner)

    def arrival(j, half, part):
        here = spot(j, half, part)
        return copy_to(here, here, s_first.at[0], r_m.at[j, half, part], partner)

    def to_sibling(j):
        return copy_to(p.at[j, 1 - co], c.at[j], s_c.at[j], r_c.at[j], sibling)

    def role(j):
        half = 1 - lax.rem(j, 2)
        toward = 1 - 2 * half
        return lax.rem(y - lax.div(j, 2) + Y, Y), half, toward

    def to_owner(j):
        _, half, toward = role(j)
        owner = lax.div(j, 2)
        side = jnp.where(lax.rem(y - owner + Y, Y) == 1, 0, 1)
        return copy_to(
            p.at[j, co], yr.at[half, side], s_y.at[j], r_y.at[half, side],
            device(x, zl, zh, owner, co),
        )

    def to_between(j):
        _, half, toward = role(j)
        return copy_to(
            p.at[j, co], far.at[half], s_y.at[j], r_far.at[half],
            device(x, zl, zh, lax.rem(y - toward + Y, Y), co),
        )

    def third(ref, index, part):
        return ref.at[index, pl.ds(part * (384 // ENDS), 384 // ENDS), :]

    def to_relay(part):
        return copy_to(
            third(t, 1 - zh, part), third(rel, 0, part), s_rel.at[part], r_rel.at[part], relay
        )

    def send_on(part):
        return copy_to(
            third(rel, 0, part), third(zb, relayed_half, part),
            s_on.at[part], r_z.at[relayed_half, part], relay_end,
        )

    def to_direct(part):
        return copy_to(
            third(t, zh, part), third(zb, zh, part), s_z.at[part], r_z.at[zh, part], direct
        )

    def goes_right(j):
        return jnp.logical_and(j <= zl, zl < 7)

    def goes_left(j):
        return jnp.logical_and(j >= zl, zl > 0)

    def step(i, carry):
        @pl.when(i < 8)
        def _():
            j = order(i)
            right, left = goes_right(j), goes_left(j)
            for part in range(PARTS):
                arrival(j, mine, part).wait_recv()

                @pl.when(right)
                def _(part=part):
                    to_right(j, part).start()

                @pl.when(left)
                def _(part=part):
                    to_left(j, part).start()

                to_partner(j, part).start()

        @pl.when(i == LAG)
        def _():
            for piece in range(PIECES):
                send_a(piece).wait_recv()
            high, low = split(a_in[...])
            a_high[1 - kind], a_low[1 - kind] = high, low

        @pl.when(jnp.logical_and(i >= LAG, i < LAG + 8))
        def _():
            j = order(i - LAG)
            for part in range(PARTS):
                arrival(j, 1 - mine, part).wait_recv()
            p[j] = product(
                a_high[...].reshape(768, 768), a_low[...].reshape(768, 768), m[j].reshape(768, 128)
            ).reshape(2, 384, 128)
            to_sibling(j).start()

        k = i - (LAG + 1)

        @pl.when(jnp.logical_and(k >= 0, k < 8))
        def _():
            j = order(k)
            to_sibling(j).wait_recv()
            p[j, co] = p[j, co] + c[j]

            distance, _, toward = role(j)

            @pl.when(distance == lax.rem(Y - toward, Y))
            def _():
                to_owner(j).start()

            @pl.when(distance == 2)
            def _():
                to_between(j).start()

        @pl.when(jnp.logical_and(k >= PASS, k < PASS + 8))
        def _():
            j = order(k - PASS)
            distance, half, toward = role(j)

            @pl.when(distance == lax.rem(Y + toward, Y))
            def _():
                copy_to(t.at[0], far.at[half], s_y.at[0], r_far.at[half], sibling).wait_recv()
                p[j, co] = p[j, co] + far[half]
                to_owner(j).start()

        @pl.when(jnp.logical_and(k >= TRAIL, k < TRAIL + 8))
        def _():
            j = order(k - TRAIL)
            half = 1 - lax.rem(j, 2)

            @pl.when(lax.div(j, 2) == y)
            def _():
                for slot in range(2):
                    copy_to(
                        t.at[0], yr.at[half, slot], s_y.at[0], r_y.at[half, slot], sibling
                    ).wait_recv()
                total = p[j, co] + (yr[half, 0] + yr[half, 1])
                here = half == zh

                @pl.when(jnp.logical_and(home, here))
                def _():
                    zb[zh] = total

                @pl.when(jnp.logical_not(jnp.logical_and(home, here)))
                def _():
                    t[half] = total

                @pl.when(jnp.logical_and(jnp.logical_not(home), here))
                def _():
                    for part in range(ENDS):
                        to_direct(part).start()

                @pl.when(jnp.logical_not(here))
                def _():
                    for part in range(ENDS):
                        to_relay(part).start()

        return carry

    lax.fori_loop(0, 8 + LAG + 1 + TRAIL, step, 0)

    for part in range(ENDS):
        to_relay(part).wait_recv()
        send_on(part).start()

    def end_arrival(half, part):
        here = third(zb, half, part)
        return copy_to(here, here, s_z.at[0], r_z.at[half, part], sibling)

    @pl.when(jnp.logical_not(home))
    def _():
        for part in range(ENDS):
            end_arrival(zh, part).wait_recv()

    for part in range(ENDS):
        end_arrival(1 - zh, part).wait_recv()

    for block in range(3):
        rows = pl.ds(block * 128, 128)
        member = mask_ref[0, block].astype(jnp.float32)
        off_ref[rows, :] = -((zb[0, rows, :] + zb[1, rows, :]) * member)

    correction = product(turned[0], turned[1], off_ref[...])
    for other in range(X):
        cs[other] = correction[other * 32 : other * 32 + 32, :]

    def corr_x(step):
        return copy_to(
            cs.at[lax.rem(x + step, X)], cx.at[step - 1], s_cx.at[step - 1], r_cx.at[step - 1],
            x_peer(step),
        )

    def corr_z(step):
        return copy_to(cz.at[zl], cz.at[zl], s_cz.at[step - 1], r_cz.at[zl], z_peer(step))

    def corr_back(step):
        return copy_to(dg.at[x], dg.at[x], s_dg.at[step - 1], r_dg.at[x], x_peer(step))

    for step_ in range(1, X):
        corr_x(step_).start()
    for step_ in range(1, X):
        corr_x(step_).wait_recv()
    cz[zl] = (cs[x] + cx[0]) + (cx[1] + cx[2])
    for step_ in range(1, ZL):
        corr_z(step_).start()
    for step_ in range(1, ZL):
        other = lax.rem(zl + step_, ZL)
        copy_to(cz.at[other], cz.at[other], s_cz.at[0], r_cz.at[other], sibling).wait_recv()
    dg[x] = ((cz[0] + cz[1]) + (cz[2] + cz[3])) + ((cz[4] + cz[5]) + (cz[6] + cz[7]))
    for step_ in range(1, X):
        corr_back(step_).start()
    for step_ in range(1, X):
        other = lax.rem(x + step_, X)
        copy_to(dg.at[other], dg.at[other], s_dg.at[0], r_dg.at[other], sibling).wait_recv()
    fetch_dinv.wait()
    for other in range(X):
        rows = pl.ds(other * 32, 32)
        diag_ref[0, rows, :] = dinv_ref[0, rows, :] - dg[other]

    for part in range(PARTS):
        first(part).wait_send()
    for piece in range(PIECES):
        send_a(piece).wait_send()

    def finish(j, carry):
        to_sibling(j).wait_send()
        for part in range(PARTS):
            to_partner(j, part).wait_send()

            @pl.when(goes_right(j))
            def _(part=part):
                to_right(j, part).wait_send()

            @pl.when(goes_left(j))
            def _(part=part):
                to_left(j, part).wait_send()

        distance, _, _ = role(j)

        @pl.when(distance == 2)
        def _():
            to_between(j).wait_send()

        @pl.when(lax.rem(distance, 2) == 1)
        def _():
            to_owner(j).wait_send()

        return carry

    lax.fori_loop(0, 8, finish, 0)
    for part in range(ENDS):
        to_relay(part).wait_send()
        send_on(part).wait_send()

    @pl.when(jnp.logical_not(home))
    def _():
        for part in range(ENDS):
            to_direct(part).wait_send()

    for step_ in range(1, X):
        corr_x(step_).wait_send()
        corr_back(step_).wait_send()
    for step_ in range(1, ZL):
        corr_z(step_).wait_send()


def on_device(inverse_part, lower_panel, struct_mask, diag_inverse):
    f32, bf16 = jnp.float32, jnp.bfloat16
    dma = pltpu.SemaphoreType.DMA
    hbm = pl.BlockSpec(memory_space=pl.ANY)
    vmem = pl.BlockSpec(memory_space=pltpu.VMEM)
    return tuple(
        pl.pallas_call(
            kernel,
            out_shape=(
                jax.ShapeDtypeStruct((384, 128), f32),
                jax.ShapeDtypeStruct((1, 128, 128), f32),
            ),
            in_specs=[hbm, hbm, pl.BlockSpec(memory_space=pltpu.SMEM), hbm],
            out_specs=(vmem, vmem),
            scratch_shapes=[
                pltpu.VMEM((384, 768), f32),
                pltpu.VMEM((384, 128), f32),
                pltpu.VMEM((1, 128, 128), f32),
                pltpu.VMEM((384, 128), f32),
                pltpu.VMEM((2, 128, 384), bf16),
                pltpu.VMEM((384, 768), f32),
                pltpu.VMEM((2, 384, 768), bf16),
                pltpu.VMEM((2, 384, 768), bf16),
                pltpu.VMEM((8, 2, 384, 128), f32),
                pltpu.VMEM((8, 2, 384, 128), f32),
                pltpu.VMEM((8, 384, 128), f32),
                pltpu.VMEM((2, 384, 128), f32),
                pltpu.VMEM((2, 2, 384, 128), f32),
                pltpu.VMEM((2, 384, 128), f32),
                pltpu.VMEM((1, 384, 128), f32),
                pltpu.VMEM((2, 384, 128), f32),
                pltpu.VMEM((4, 32, 128), f32),
                pltpu.VMEM((3, 32, 128), f32),
                pltpu.VMEM((8, 32, 128), f32),
                pltpu.VMEM((4, 32, 128), f32),
                dma((3,)), dma((PIECES,)), dma((PIECES,)), dma((PARTS,)),
                dma((8, PARTS)), dma((8, PARTS)), dma((8, PARTS)), dma((8, 2, PARTS)),
                dma((8,)), dma((8,)), dma((8,)), dma((2, 2)), dma((2,)),
                dma((ENDS,)), dma((ENDS,)), dma((ENDS,)), dma((ENDS,)), dma((2, ENDS)),
                dma((3,)), dma((3,)), dma((7,)), dma((8,)), dma((3,)), dma((4,)),
            ],
            compiler_params=pltpu.CompilerParams(
                collective_id=0, has_side_effects=True, vmem_limit_bytes=63 * 1024 * 1024
            ),
            cost_estimate=pl.CostEstimate(
                flops=2 * 3 * 384 * 768 * 2048, bytes_accessed=4_000_000, transcendentals=0
            ),
        )(inverse_part, lower_panel, struct_mask, diag_inverse)
    )


def solution(mesh):
    return jax.shard_map(
        on_device,
        mesh=mesh,
        in_specs=(P("prow", "pcol"), P("prow", "pcol"), P("pcol", "prow"), P("pcol", None, None)),
        out_specs=(P("prow", "pcol"), P("pcol", None, None)),
        check_vma=False,
    )
```

```python
import jax
import jax.numpy as jnp
from jax import lax
from jax.experimental import pallas as pl
from jax.experimental.pallas import tpu as pltpu
from jax.sharding import PartitionSpec as P

MESH = pl.DeviceIdType.MESH
X, ZL, ZH, Y = 4, 8, 2, 4
PIECES = 3
PARTS = 4
LAG = 2
PASS = 2
TRAIL = 4


def split(value):
    high = value.astype(jnp.bfloat16)
    return high, (value - high.astype(jnp.float32)).astype(jnp.bfloat16)


def product(left_high, left_low, right):
    high, low = split(right)
    width = right.shape[1]
    both = jnp.dot(
        left_high, jnp.concatenate([high, low], axis=1), preferred_element_type=jnp.float32
    )
    rest = jnp.dot(left_low, high, preferred_element_type=jnp.float32)
    return both[:, :width] + (both[:, width:] + rest)


def copy_to(src, dst, send, recv, device):
    return pltpu.make_async_remote_copy(
        src_ref=src, dst_ref=dst, send_sem=send, recv_sem=recv,
        device_id=device, device_id_type=MESH,
    )


def kernel(
    a_hbm, l_hbm, mask_ref, dinv_hbm, off_ref, diag_ref,
    a_ref, l_ref, dinv_ref, masked, turned, a_in, a_high, a_low, m, p, c, far, yr, t, zb, cs, cx, cz, dg,
    fetch, s_a, r_a, s_first, s_right, s_left, s_x, r_m, s_c, r_c, s_y, r_y, r_far, s_z, r_z,
    s_cx, r_cx, s_cz, r_cz, s_dg, r_dg,
):
    row, col = lax.axis_index("prow"), lax.axis_index("pcol")
    x, zl = lax.div(row, ZL), lax.rem(row, ZL)
    zh, y, co = lax.div(col, 8), lax.rem(lax.div(col, 2), Y), lax.rem(col, 2)

    def device(x, zl, zh, y, co):
        return (x * ZL + zl, zh * 8 + y * 2 + co)

    kind = lax.rem(lax.div(x + 1, 2), 2)
    x_a, x_m = x + 1 - 2 * lax.rem(x, 2), 3 - x
    home = co == kind
    mine = lax.rem(lax.div(x, 2) + zh, 2)

    first_to = device(
        lax.rem(zl + lax.div(x, 2), 2) * 2 + lax.rem(lax.rem(zl + lax.div(x, 2), 2) + co, 2),
        2 * y + 1 - zh,
        lax.div(x, 2), 2 * lax.rem(x, 2) + lax.div(zl, 4), lax.rem(lax.div(zl, 2), 2),
    )
    first_slot = 2 * y + 1 - zh
    first_half = lax.rem(zl, 2)
    first_from = device(
        2 * zh + lax.div(y, 2),
        4 * lax.rem(y, 2) + 2 * co + mine,
        1 - lax.rem(zl, 2), lax.div(zl, 2), kind,
    )
    sibling = device(x, zl, zh, y, 1 - co)
    partner = device(x_m, zl, zh, y, co)
    a_partner = device(x_a, zl, zh, y, co)

    def x_peer(step):
        return device(lax.rem(x + step, X), zl, zh, y, co)

    def z_peer(step):
        return device(x, lax.rem(zl + step, ZL), zh, y, co)

    def y_peer(step):
        return device(x, zl, zh, lax.rem(y + step, Y), co)

    def end_peer(half):
        return device(jnp.where(home, x, x_a), zl, half, y, kind)

    fetch_l = pltpu.make_async_copy(l_hbm, l_ref, fetch.at[0])
    fetch_a = pltpu.make_async_copy(a_hbm, a_ref, fetch.at[1])
    fetch_dinv = pltpu.make_async_copy(dinv_hbm, dinv_ref, fetch.at[2])
    fetch_l.start()
    fetch_a.start()
    fetch_dinv.start()

    barrier = pltpu.get_barrier_semaphore()

    def greet(who):
        pl.semaphore_signal(barrier, inc=1, device_id=who, device_id_type=MESH)

    greet(first_from)
    greet(sibling)
    for step in range(1, X):
        greet(x_peer(step))
    for step in range(1, Y):
        greet(y_peer(step))
    for step in range(1, ZL):
        greet(z_peer(step))
    greet(end_peer(1 - zh))

    @pl.when(jnp.logical_not(home))
    def _():
        greet(end_peer(zh))

    fetch_l.wait()
    for block in range(3):
        rows = pl.ds(block * 128, 128)
        member = mask_ref[0, block].astype(jnp.float32)
        masked[rows, :] = l_ref[rows, :] * member

    pl.semaphore_wait(barrier, jnp.where(home, 16, 17))

    def spot(j, half, part):
        return m.at[j, half, pl.ds(part * (384 // PARTS), 384 // PARTS), :]

    def first(part):
        return copy_to(
            masked.at[pl.ds(part * (384 // PARTS), 384 // PARTS), :],
            spot(first_slot, first_half, part),
            s_first.at[part], r_m.at[first_slot, first_half, part], first_to,
        )

    for part in range(PARTS):
        first(part).start()

    def send_a(piece):
        rows = pl.ds(piece * 128, 128)
        return copy_to(
            a_ref.at[rows, :], a_in.at[rows, :], s_a.at[piece], r_a.at[piece], a_partner
        )

    fetch_a.wait()
    for piece in range(PIECES):
        send_a(piece).start()
    high, low = split(a_ref[...])
    a_high[kind], a_low[kind] = high, low
    high, low = split(masked[...].T)
    turned[0], turned[1] = high, low

    def order(i):
        half = lax.div(i + 1, 2)
        near = jnp.where(lax.rem(i, 2) == 1, zl - half, zl + half)
        far = jnp.where(zl <= 3, i, 7 - i)
        return jnp.where(i <= 2 * jnp.minimum(zl, 7 - zl), near, far)

    def to_right(j, part):
        here = spot(j, mine, part)
        return copy_to(
            here, here, s_right.at[j, part], r_m.at[j, mine, part],
            device(x, jnp.minimum(zl + 1, 7), zh, y, co),
        )

    def to_left(j, part):
        here = spot(j, mine, part)
        return copy_to(
            here, here, s_left.at[j, part], r_m.at[j, mine, part],
            device(x, jnp.maximum(zl - 1, 0), zh, y, co),
        )

    def to_partner(j, part):
        here = spot(j, mine, part)
        return copy_to(here, here, s_x.at[j, part], r_m.at[j, mine, part], partner)

    def arrival(j, half, part):
        here = spot(j, half, part)
        return copy_to(here, here, s_first.at[0], r_m.at[j, half, part], partner)

    def to_sibling(j):
        return copy_to(p.at[j, 1 - co], c.at[j], s_c.at[j], r_c.at[j], sibling)

    def role(j):
        half = 1 - lax.rem(j, 2)
        toward = 1 - 2 * half
        return lax.rem(y - lax.div(j, 2) + Y, Y), half, toward

    def to_owner(j):
        _, half, toward = role(j)
        owner = lax.div(j, 2)
        side = jnp.where(lax.rem(y - owner + Y, Y) == 1, 0, 1)
        return copy_to(
            p.at[j, co], yr.at[half, side], s_y.at[j], r_y.at[half, side],
            device(x, zl, zh, owner, co),
        )

    def to_between(j):
        _, half, toward = role(j)
        return copy_to(
            p.at[j, co], far.at[half], s_y.at[j], r_far.at[half],
            device(x, zl, zh, lax.rem(y - toward + Y, Y), co),
        )

    def to_end(half):
        return copy_to(t.at[half], zb.at[zh], s_z.at[half], r_z.at[zh], end_peer(half))

    def goes_right(j):
        return jnp.logical_and(j <= zl, zl < 7)

    def goes_left(j):
        return jnp.logical_and(j >= zl, zl > 0)

    def step(i, carry):
        @pl.when(i < 8)
        def _():
            j = order(i)
            right, left = goes_right(j), goes_left(j)
            for part in range(PARTS):
                arrival(j, mine, part).wait_recv()

                @pl.when(right)
                def _(part=part):
                    to_right(j, part).start()

                @pl.when(left)
                def _(part=part):
                    to_left(j, part).start()

                to_partner(j, part).start()

        @pl.when(i == LAG)
        def _():
            for piece in range(PIECES):
                send_a(piece).wait_recv()
            high, low = split(a_in[...])
            a_high[1 - kind], a_low[1 - kind] = high, low

        @pl.when(jnp.logical_and(i >= LAG, i < LAG + 8))
        def _():
            j = order(i - LAG)
            for part in range(PARTS):
                arrival(j, 1 - mine, part).wait_recv()
            p[j] = product(
                a_high[...].reshape(768, 768), a_low[...].reshape(768, 768), m[j].reshape(768, 128)
            ).reshape(2, 384, 128)
            to_sibling(j).start()

        k = i - (LAG + 1)

        @pl.when(jnp.logical_and(k >= 0, k < 8))
        def _():
            j = order(k)
            to_sibling(j).wait_recv()
            p[j, co] = p[j, co] + c[j]

            distance, _, toward = role(j)

            @pl.when(distance == lax.rem(Y - toward, Y))
            def _():
                to_owner(j).start()

            @pl.when(distance == 2)
            def _():
                to_between(j).start()

        @pl.when(jnp.logical_and(k >= PASS, k < PASS + 8))
        def _():
            j = order(k - PASS)
            distance, half, toward = role(j)

            @pl.when(distance == lax.rem(Y + toward, Y))
            def _():
                copy_to(t.at[0], far.at[half], s_y.at[0], r_far.at[half], sibling).wait_recv()
                p[j, co] = p[j, co] + far[half]
                to_owner(j).start()

        @pl.when(jnp.logical_and(k >= TRAIL, k < TRAIL + 8))
        def _():
            j = order(k - TRAIL)
            half = 1 - lax.rem(j, 2)

            @pl.when(lax.div(j, 2) == y)
            def _():
                for slot in range(2):
                    copy_to(
                        t.at[0], yr.at[half, slot], s_y.at[0], r_y.at[half, slot], sibling
                    ).wait_recv()
                total = p[j, co] + (yr[half, 0] + yr[half, 1])
                stays = jnp.logical_and(home, half == zh)

                @pl.when(stays)
                def _():
                    zb[zh] = total

                @pl.when(jnp.logical_not(stays))
                def _():
                    t[half] = total
                    to_end(half).start()

        return carry

    lax.fori_loop(0, 8 + LAG + 1 + TRAIL, step, 0)

    for part in range(PARTS):
        first(part).wait_send()
    for piece in range(PIECES):
        send_a(piece).wait_send()

    def finish(j, carry):
        to_sibling(j).wait_send()
        for part in range(PARTS):
            to_partner(j, part).wait_send()

            @pl.when(goes_right(j))
            def _(part=part):
                to_right(j, part).wait_send()

            @pl.when(goes_left(j))
            def _(part=part):
                to_left(j, part).wait_send()

        distance, _, _ = role(j)

        @pl.when(distance == 2)
        def _():
            to_between(j).wait_send()

        @pl.when(lax.rem(distance, 2) == 1)
        def _():
            to_owner(j).wait_send()

        return carry

    lax.fori_loop(0, 8, finish, 0)

    def end_arrival(half):
        return copy_to(t.at[0], zb.at[half], s_z.at[0], r_z.at[half], sibling)

    end_arrival(1 - zh).wait_recv()

    @pl.when(jnp.logical_not(home))
    def _():
        end_arrival(zh).wait_recv()

    for block in range(3):
        rows = pl.ds(block * 128, 128)
        member = mask_ref[0, block].astype(jnp.float32)
        off_ref[rows, :] = -((zb[0, rows, :] + zb[1, rows, :]) * member)

    correction = product(turned[0], turned[1], off_ref[...])
    for other in range(X):
        cs[other] = correction[other * 32 : other * 32 + 32, :]

    def corr_x(step):
        return copy_to(
            cs.at[lax.rem(x + step, X)], cx.at[step - 1], s_cx.at[step - 1], r_cx.at[step - 1],
            x_peer(step),
        )

    def corr_z(step):
        return copy_to(cz.at[zl], cz.at[zl], s_cz.at[step - 1], r_cz.at[zl], z_peer(step))

    def corr_back(step):
        return copy_to(dg.at[x], dg.at[x], s_dg.at[step - 1], r_dg.at[x], x_peer(step))

    for step_ in range(1, X):
        corr_x(step_).start()
    for step_ in range(1, X):
        corr_x(step_).wait_recv()
    cz[zl] = (cs[x] + cx[0]) + (cx[1] + cx[2])
    for step_ in range(1, ZL):
        corr_z(step_).start()
    for step_ in range(1, ZL):
        other = lax.rem(zl + step_, ZL)
        copy_to(cz.at[other], cz.at[other], s_cz.at[0], r_cz.at[other], sibling).wait_recv()
    dg[x] = ((cz[0] + cz[1]) + (cz[2] + cz[3])) + ((cz[4] + cz[5]) + (cz[6] + cz[7]))
    for step_ in range(1, X):
        corr_back(step_).start()
    for step_ in range(1, X):
        other = lax.rem(x + step_, X)
        copy_to(dg.at[other], dg.at[other], s_dg.at[0], r_dg.at[other], sibling).wait_recv()
    fetch_dinv.wait()
    for other in range(X):
        rows = pl.ds(other * 32, 32)
        diag_ref[0, rows, :] = dinv_ref[0, rows, :] - dg[other]

    to_end(1 - zh).wait_send()

    @pl.when(jnp.logical_not(home))
    def _():
        to_end(zh).wait_send()

    for step_ in range(1, X):
        corr_x(step_).wait_send()
        corr_back(step_).wait_send()
    for step_ in range(1, ZL):
        corr_z(step_).wait_send()


def on_device(inverse_part, lower_panel, struct_mask, diag_inverse):
    f32, bf16 = jnp.float32, jnp.bfloat16
    dma = pltpu.SemaphoreType.DMA
    hbm = pl.BlockSpec(memory_space=pl.ANY)
    vmem = pl.BlockSpec(memory_space=pltpu.VMEM)
    return tuple(
        pl.pallas_call(
            kernel,
            out_shape=(
                jax.ShapeDtypeStruct((384, 128), f32),
                jax.ShapeDtypeStruct((1, 128, 128), f32),
            ),
            in_specs=[hbm, hbm, pl.BlockSpec(memory_space=pltpu.SMEM), hbm],
            out_specs=(vmem, vmem),
            scratch_shapes=[
                pltpu.VMEM((384, 768), f32),
                pltpu.VMEM((384, 128), f32),
                pltpu.VMEM((1, 128, 128), f32),
                pltpu.VMEM((384, 128), f32),
                pltpu.VMEM((2, 128, 384), bf16),
                pltpu.VMEM((384, 768), f32),
                pltpu.VMEM((2, 384, 768), bf16),
                pltpu.VMEM((2, 384, 768), bf16),
                pltpu.VMEM((8, 2, 384, 128), f32),
                pltpu.VMEM((8, 2, 384, 128), f32),
                pltpu.VMEM((8, 384, 128), f32),
                pltpu.VMEM((2, 384, 128), f32),
                pltpu.VMEM((2, 2, 384, 128), f32),
                pltpu.VMEM((2, 384, 128), f32),
                pltpu.VMEM((2, 384, 128), f32),
                pltpu.VMEM((4, 32, 128), f32),
                pltpu.VMEM((3, 32, 128), f32),
                pltpu.VMEM((8, 32, 128), f32),
                pltpu.VMEM((4, 32, 128), f32),
                dma((3,)), dma((PIECES,)), dma((PIECES,)), dma((PARTS,)),
                dma((8, PARTS)), dma((8, PARTS)), dma((8, PARTS)), dma((8, 2, PARTS)),
                dma((8,)), dma((8,)), dma((8,)), dma((2, 2)), dma((2,)), dma((2,)), dma((2,)),
                dma((3,)), dma((3,)), dma((7,)), dma((8,)), dma((3,)), dma((4,)),
            ],
            compiler_params=pltpu.CompilerParams(
                collective_id=0, has_side_effects=True, vmem_limit_bytes=63 * 1024 * 1024
            ),
            cost_estimate=pl.CostEstimate(
                flops=2 * 3 * 384 * 768 * 2048, bytes_accessed=4_000_000, transcendentals=0
            ),
        )(inverse_part, lower_panel, struct_mask, diag_inverse)
    )


def solution(mesh):
    return jax.shard_map(
        on_device,
        mesh=mesh,
        in_specs=(P("prow", "pcol"), P("prow", "pcol"), P("pcol", "prow"), P("pcol", None, None)),
        out_specs=(P("prow", "pcol"), P("pcol", None, None)),
        check_vma=False,
    )
```

```python
import jax
import jax.numpy as jnp
from jax import lax
from jax.experimental import pallas as pl
from jax.experimental.pallas import tpu as pltpu
from jax.sharding import PartitionSpec as P

MESH = pl.DeviceIdType.MESH
X, ZL, ZH, Y = 4, 8, 2, 4
PIECES = 3
PARTS = 2
LAG = 3
PASS = 2
TRAIL = 4


def split(value):
    high = value.astype(jnp.bfloat16)
    return high, (value - high.astype(jnp.float32)).astype(jnp.bfloat16)


def product(left_high, left_low, right):
    high, low = split(right)
    width = right.shape[1]
    both = jnp.dot(
        left_high, jnp.concatenate([high, low], axis=1), preferred_element_type=jnp.float32
    )
    rest = jnp.dot(left_low, high, preferred_element_type=jnp.float32)
    return both[:, :width] + (both[:, width:] + rest)


def copy_to(src, dst, send, recv, device):
    return pltpu.make_async_remote_copy(
        src_ref=src, dst_ref=dst, send_sem=send, recv_sem=recv,
        device_id=device, device_id_type=MESH,
    )


def kernel(
    a_hbm, l_hbm, mask_ref, dinv_hbm, off_ref, diag_ref,
    a_ref, l_ref, dinv_ref, masked, turned, a_in, a_high, a_low, m, p, c, far, yr, t, zb, cs, cx, cz, dg,
    fetch, s_a, r_a, s_first, s_right, s_left, s_x, r_m, s_c, r_c, s_y, r_y, r_far, s_z, r_z,
    s_cx, r_cx, s_cz, r_cz, s_dg, r_dg,
):
    row, col = lax.axis_index("prow"), lax.axis_index("pcol")
    x, zl = lax.div(row, ZL), lax.rem(row, ZL)
    zh, y, co = lax.div(col, 8), lax.rem(lax.div(col, 2), Y), lax.rem(col, 2)

    def device(x, zl, zh, y, co):
        return (x * ZL + zl, zh * 8 + y * 2 + co)

    kind = lax.rem(lax.div(x + 1, 2), 2)
    x_a, x_m = x + 1 - 2 * lax.rem(x, 2), 3 - x
    home = co == kind
    mine = lax.rem(lax.div(x, 2) + zh, 2)

    first_to = device(
        lax.rem(zl + lax.div(x, 2), 2) * 2 + lax.rem(lax.rem(zl + lax.div(x, 2), 2) + co, 2),
        2 * y + 1 - zh,
        lax.div(x, 2), 2 * lax.rem(x, 2) + lax.div(zl, 4), lax.rem(lax.div(zl, 2), 2),
    )
    first_slot = 2 * y + 1 - zh
    first_half = lax.rem(zl, 2)
    first_from = device(
        2 * zh + lax.div(y, 2),
        4 * lax.rem(y, 2) + 2 * co + mine,
        1 - lax.rem(zl, 2), lax.div(zl, 2), kind,
    )
    sibling = device(x, zl, zh, y, 1 - co)
    partner = device(x_m, zl, zh, y, co)
    a_partner = device(x_a, zl, zh, y, co)

    def x_peer(step):
        return device(lax.rem(x + step, X), zl, zh, y, co)

    def z_peer(step):
        return device(x, lax.rem(zl + step, ZL), zh, y, co)

    def y_peer(step):
        return device(x, zl, zh, lax.rem(y + step, Y), co)

    def end_peer(half):
        return device(jnp.where(home, x, x_a), zl, half, y, kind)

    fetch_l = pltpu.make_async_copy(l_hbm, l_ref, fetch.at[0])
    fetch_a = pltpu.make_async_copy(a_hbm, a_ref, fetch.at[1])
    fetch_dinv = pltpu.make_async_copy(dinv_hbm, dinv_ref, fetch.at[2])
    fetch_l.start()
    fetch_a.start()
    fetch_dinv.start()

    barrier = pltpu.get_barrier_semaphore()

    def greet(who):
        pl.semaphore_signal(barrier, inc=1, device_id=who, device_id_type=MESH)

    greet(first_from)
    greet(sibling)
    for step in range(1, X):
        greet(x_peer(step))
    for step in range(1, Y):
        greet(y_peer(step))
    for step in range(1, ZL):
        greet(z_peer(step))
    greet(end_peer(1 - zh))

    @pl.when(jnp.logical_not(home))
    def _():
        greet(end_peer(zh))

    fetch_l.wait()
    for block in range(3):
        rows = pl.ds(block * 128, 128)
        member = mask_ref[0, block].astype(jnp.float32)
        masked[rows, :] = l_ref[rows, :] * member

    pl.semaphore_wait(barrier, jnp.where(home, 16, 17))

    def spot(j, half, part):
        return m.at[j, half, pl.ds(part * (384 // PARTS), 384 // PARTS), :]

    def first(part):
        return copy_to(
            masked.at[pl.ds(part * (384 // PARTS), 384 // PARTS), :],
            spot(first_slot, first_half, part),
            s_first.at[part], r_m.at[first_slot, first_half, part], first_to,
        )

    for part in range(PARTS):
        first(part).start()

    def send_a(piece):
        rows = pl.ds(piece * 128, 128)
        return copy_to(
            a_ref.at[rows, :], a_in.at[rows, :], s_a.at[piece], r_a.at[piece], a_partner
        )

    fetch_a.wait()
    for piece in range(PIECES):
        send_a(piece).start()
    high, low = split(a_ref[...])
    a_high[kind], a_low[kind] = high, low
    high, low = split(masked[...].T)
    turned[0], turned[1] = high, low

    def order(i):
        half = lax.div(i + 1, 2)
        near = jnp.where(lax.rem(i, 2) == 1, zl - half, zl + half)
        far = jnp.where(zl <= 3, i, 7 - i)
        return jnp.where(i <= 2 * jnp.minimum(zl, 7 - zl), near, far)

    def to_right(j, part):
        here = spot(j, mine, part)
        return copy_to(
            here, here, s_right.at[j, part], r_m.at[j, mine, part],
            device(x, jnp.minimum(zl + 1, 7), zh, y, co),
        )

    def to_left(j, part):
        here = spot(j, mine, part)
        return copy_to(
            here, here, s_left.at[j, part], r_m.at[j, mine, part],
            device(x, jnp.maximum(zl - 1, 0), zh, y, co),
        )

    def to_partner(j, part):
        here = spot(j, mine, part)
        return copy_to(here, here, s_x.at[j, part], r_m.at[j, mine, part], partner)

    def arrival(j, half, part):
        here = spot(j, half, part)
        return copy_to(here, here, s_first.at[0], r_m.at[j, half, part], partner)

    def to_sibling(j):
        return copy_to(p.at[j, 1 - co], c.at[j], s_c.at[j], r_c.at[j], sibling)

    def role(j):
        half = 1 - lax.rem(j, 2)
        toward = 1 - 2 * half
        return lax.rem(y - lax.div(j, 2) + Y, Y), half, toward

    def to_owner(j):
        _, half, toward = role(j)
        owner = lax.div(j, 2)
        side = jnp.where(lax.rem(y - owner + Y, Y) == 1, 0, 1)
        return copy_to(
            p.at[j, co], yr.at[half, side], s_y.at[j], r_y.at[half, side],
            device(x, zl, zh, owner, co),
        )

    def to_between(j):
        _, half, toward = role(j)
        return copy_to(
            p.at[j, co], far.at[half], s_y.at[j], r_far.at[half],
            device(x, zl, zh, lax.rem(y - toward + Y, Y), co),
        )

    def to_end(half):
        return copy_to(t.at[half], zb.at[zh], s_z.at[half], r_z.at[zh], end_peer(half))

    def goes_right(j):
        return jnp.logical_and(j <= zl, zl < 7)

    def goes_left(j):
        return jnp.logical_and(j >= zl, zl > 0)

    def step(i, carry):
        @pl.when(i < 8)
        def _():
            j = order(i)
            right, left = goes_right(j), goes_left(j)
            for part in range(PARTS):
                arrival(j, mine, part).wait_recv()

                @pl.when(right)
                def _(part=part):
                    to_right(j, part).start()

                @pl.when(left)
                def _(part=part):
                    to_left(j, part).start()

                to_partner(j, part).start()

        @pl.when(i == LAG)
        def _():
            for piece in range(PIECES):
                send_a(piece).wait_recv()
            high, low = split(a_in[...])
            a_high[1 - kind], a_low[1 - kind] = high, low

        @pl.when(jnp.logical_and(i >= LAG, i < LAG + 8))
        def _():
            j = order(i - LAG)
            for part in range(PARTS):
                arrival(j, 1 - mine, part).wait_recv()
            p[j] = product(
                a_high[...].reshape(768, 768), a_low[...].reshape(768, 768), m[j].reshape(768, 128)
            ).reshape(2, 384, 128)
            to_sibling(j).start()

        k = i - (LAG + 1)

        @pl.when(jnp.logical_and(k >= 0, k < 8))
        def _():
            j = order(k)
            to_sibling(j).wait_recv()
            p[j, co] = p[j, co] + c[j]

            distance, _, toward = role(j)

            @pl.when(distance == lax.rem(Y - toward, Y))
            def _():
                to_owner(j).start()

            @pl.when(distance == 2)
            def _():
                to_between(j).start()

        @pl.when(jnp.logical_and(k >= PASS, k < PASS + 8))
        def _():
            j = order(k - PASS)
            distance, half, toward = role(j)

            @pl.when(distance == lax.rem(Y + toward, Y))
            def _():
                copy_to(t.at[0], far.at[half], s_y.at[0], r_far.at[half], sibling).wait_recv()
                p[j, co] = p[j, co] + far[half]
                to_owner(j).start()

        @pl.when(jnp.logical_and(k >= TRAIL, k < TRAIL + 8))
        def _():
            j = order(k - TRAIL)
            half = 1 - lax.rem(j, 2)

            @pl.when(lax.div(j, 2) == y)
            def _():
                for slot in range(2):
                    copy_to(
                        t.at[0], yr.at[half, slot], s_y.at[0], r_y.at[half, slot], sibling
                    ).wait_recv()
                total = p[j, co] + (yr[half, 0] + yr[half, 1])
                stays = jnp.logical_and(home, half == zh)

                @pl.when(stays)
                def _():
                    zb[zh] = total

                @pl.when(jnp.logical_not(stays))
                def _():
                    t[half] = total
                    to_end(half).start()

        return carry

    lax.fori_loop(0, 8 + LAG + 1 + TRAIL, step, 0)

    for part in range(PARTS):
        first(part).wait_send()
    for piece in range(PIECES):
        send_a(piece).wait_send()

    def finish(j, carry):
        to_sibling(j).wait_send()
        for part in range(PARTS):
            to_partner(j, part).wait_send()

            @pl.when(goes_right(j))
            def _(part=part):
                to_right(j, part).wait_send()

            @pl.when(goes_left(j))
            def _(part=part):
                to_left(j, part).wait_send()

        distance, _, _ = role(j)

        @pl.when(distance == 2)
        def _():
            to_between(j).wait_send()

        @pl.when(lax.rem(distance, 2) == 1)
        def _():
            to_owner(j).wait_send()

        return carry

    lax.fori_loop(0, 8, finish, 0)

    def end_arrival(half):
        return copy_to(t.at[0], zb.at[half], s_z.at[0], r_z.at[half], sibling)

    end_arrival(1 - zh).wait_recv()

    @pl.when(jnp.logical_not(home))
    def _():
        end_arrival(zh).wait_recv()

    for block in range(3):
        rows = pl.ds(block * 128, 128)
        member = mask_ref[0, block].astype(jnp.float32)
        off_ref[rows, :] = -((zb[0, rows, :] + zb[1, rows, :]) * member)

    correction = product(turned[0], turned[1], off_ref[...])
    for other in range(X):
        cs[other] = correction[other * 32 : other * 32 + 32, :]

    def corr_x(step):
        return copy_to(
            cs.at[lax.rem(x + step, X)], cx.at[step - 1], s_cx.at[step - 1], r_cx.at[step - 1],
            x_peer(step),
        )

    def corr_z(step):
        return copy_to(cz.at[zl], cz.at[zl], s_cz.at[step - 1], r_cz.at[zl], z_peer(step))

    def corr_back(step):
        return copy_to(dg.at[x], dg.at[x], s_dg.at[step - 1], r_dg.at[x], x_peer(step))

    for step_ in range(1, X):
        corr_x(step_).start()
    for step_ in range(1, X):
        corr_x(step_).wait_recv()
    cz[zl] = (cs[x] + cx[0]) + (cx[1] + cx[2])
    for step_ in range(1, ZL):
        corr_z(step_).start()
    for step_ in range(1, ZL):
        other = lax.rem(zl + step_, ZL)
        copy_to(cz.at[other], cz.at[other], s_cz.at[0], r_cz.at[other], sibling).wait_recv()
    dg[x] = ((cz[0] + cz[1]) + (cz[2] + cz[3])) + ((cz[4] + cz[5]) + (cz[6] + cz[7]))
    for step_ in range(1, X):
        corr_back(step_).start()
    for step_ in range(1, X):
        other = lax.rem(x + step_, X)
        copy_to(dg.at[other], dg.at[other], s_dg.at[0], r_dg.at[other], sibling).wait_recv()
    fetch_dinv.wait()
    for other in range(X):
        rows = pl.ds(other * 32, 32)
        diag_ref[0, rows, :] = dinv_ref[0, rows, :] - dg[other]

    to_end(1 - zh).wait_send()

    @pl.when(jnp.logical_not(home))
    def _():
        to_end(zh).wait_send()

    for step_ in range(1, X):
        corr_x(step_).wait_send()
        corr_back(step_).wait_send()
    for step_ in range(1, ZL):
        corr_z(step_).wait_send()


def on_device(inverse_part, lower_panel, struct_mask, diag_inverse):
    f32, bf16 = jnp.float32, jnp.bfloat16
    dma = pltpu.SemaphoreType.DMA
    hbm = pl.BlockSpec(memory_space=pl.ANY)
    vmem = pl.BlockSpec(memory_space=pltpu.VMEM)
    return tuple(
        pl.pallas_call(
            kernel,
            out_shape=(
                jax.ShapeDtypeStruct((384, 128), f32),
                jax.ShapeDtypeStruct((1, 128, 128), f32),
            ),
            in_specs=[hbm, hbm, pl.BlockSpec(memory_space=pltpu.SMEM), hbm],
            out_specs=(vmem, vmem),
            scratch_shapes=[
                pltpu.VMEM((384, 768), f32),
                pltpu.VMEM((384, 128), f32),
                pltpu.VMEM((1, 128, 128), f32),
                pltpu.VMEM((384, 128), f32),
                pltpu.VMEM((2, 128, 384), bf16),
                pltpu.VMEM((384, 768), f32),
                pltpu.VMEM((2, 384, 768), bf16),
                pltpu.VMEM((2, 384, 768), bf16),
                pltpu.VMEM((8, 2, 384, 128), f32),
                pltpu.VMEM((8, 2, 384, 128), f32),
                pltpu.VMEM((8, 384, 128), f32),
                pltpu.VMEM((2, 384, 128), f32),
                pltpu.VMEM((2, 2, 384, 128), f32),
                pltpu.VMEM((2, 384, 128), f32),
                pltpu.VMEM((2, 384, 128), f32),
                pltpu.VMEM((4, 32, 128), f32),
                pltpu.VMEM((3, 32, 128), f32),
                pltpu.VMEM((8, 32, 128), f32),
                pltpu.VMEM((4, 32, 128), f32),
                dma((3,)), dma((PIECES,)), dma((PIECES,)), dma((PARTS,)),
                dma((8, PARTS)), dma((8, PARTS)), dma((8, PARTS)), dma((8, 2, PARTS)),
                dma((8,)), dma((8,)), dma((8,)), dma((2, 2)), dma((2,)), dma((2,)), dma((2,)),
                dma((3,)), dma((3,)), dma((7,)), dma((8,)), dma((3,)), dma((4,)),
            ],
            compiler_params=pltpu.CompilerParams(
                collective_id=0, has_side_effects=True, vmem_limit_bytes=63 * 1024 * 1024
            ),
            cost_estimate=pl.CostEstimate(
                flops=2 * 3 * 384 * 768 * 2048, bytes_accessed=4_000_000, transcendentals=0
            ),
        )(inverse_part, lower_panel, struct_mask, diag_inverse)
    )


def solution(mesh):
    return jax.shard_map(
        on_device,
        mesh=mesh,
        in_specs=(P("prow", "pcol"), P("prow", "pcol"), P("pcol", "prow"), P("pcol", None, None)),
        out_specs=(P("prow", "pcol"), P("pcol", None, None)),
        check_vma=False,
    )
```

```python
import jax
import jax.numpy as jnp
from jax import lax
from jax.experimental import pallas as pl
from jax.experimental.pallas import tpu as pltpu
from jax.sharding import PartitionSpec as P

MESH = pl.DeviceIdType.MESH
X, ZL, ZH, Y = 4, 8, 2, 4
PIECES = 3
PARTS = 3
LAG = 3
PASS = 2
TRAIL = 4


def split(value):
    high = value.astype(jnp.bfloat16)
    return high, (value - high.astype(jnp.float32)).astype(jnp.bfloat16)


def product(left_high, left_low, right):
    high, low = split(right)
    width = right.shape[1]
    both = jnp.dot(
        left_high, jnp.concatenate([high, low], axis=1), preferred_element_type=jnp.float32
    )
    rest = jnp.dot(left_low, high, preferred_element_type=jnp.float32)
    return both[:, :width] + (both[:, width:] + rest)


def copy_to(src, dst, send, recv, device):
    return pltpu.make_async_remote_copy(
        src_ref=src, dst_ref=dst, send_sem=send, recv_sem=recv,
        device_id=device, device_id_type=MESH,
    )


def kernel(
    a_hbm, l_hbm, mask_ref, dinv_hbm, off_ref, diag_ref,
    a_ref, l_ref, dinv_ref, masked, turned, a_in, a_high, a_low, m, p, c, far, yr, t, zb, cs, cx, cz, dg,
    fetch, s_a, r_a, s_first, s_right, s_left, s_x, r_m, s_c, r_c, s_y, r_y, r_far, s_z, r_z,
    s_cx, r_cx, s_cz, r_cz, s_dg, r_dg,
):
    row, col = lax.axis_index("prow"), lax.axis_index("pcol")
    x, zl = lax.div(row, ZL), lax.rem(row, ZL)
    zh, y, co = lax.div(col, 8), lax.rem(lax.div(col, 2), Y), lax.rem(col, 2)

    def device(x, zl, zh, y, co):
        return (x * ZL + zl, zh * 8 + y * 2 + co)

    kind = lax.rem(lax.div(x + 1, 2), 2)
    x_a, x_m = x + 1 - 2 * lax.rem(x, 2), 3 - x
    home = co == kind
    mine = lax.rem(lax.div(x, 2) + zh, 2)

    first_to = device(
        lax.rem(zl + lax.div(x, 2), 2) * 2 + lax.rem(lax.rem(zl + lax.div(x, 2), 2) + co, 2),
        2 * y + 1 - zh,
        lax.div(x, 2), 2 * lax.rem(x, 2) + lax.div(zl, 4), lax.rem(lax.div(zl, 2), 2),
    )
    first_slot = 2 * y + 1 - zh
    first_half = lax.rem(zl, 2)
    first_from = device(
        2 * zh + lax.div(y, 2),
        4 * lax.rem(y, 2) + 2 * co + mine,
        1 - lax.rem(zl, 2), lax.div(zl, 2), kind,
    )
    sibling = device(x, zl, zh, y, 1 - co)
    partner = device(x_m, zl, zh, y, co)
    a_partner = device(x_a, zl, zh, y, co)

    def x_peer(step):
        return device(lax.rem(x + step, X), zl, zh, y, co)

    def z_peer(step):
        return device(x, lax.rem(zl + step, ZL), zh, y, co)

    def y_peer(step):
        return device(x, zl, zh, lax.rem(y + step, Y), co)

    def end_peer(half):
        return device(jnp.where(home, x, x_a), zl, half, y, kind)

    fetch_l = pltpu.make_async_copy(l_hbm, l_ref, fetch.at[0])
    fetch_a = pltpu.make_async_copy(a_hbm, a_ref, fetch.at[1])
    fetch_dinv = pltpu.make_async_copy(dinv_hbm, dinv_ref, fetch.at[2])
    fetch_l.start()
    fetch_a.start()
    fetch_dinv.start()

    barrier = pltpu.get_barrier_semaphore()

    def greet(who):
        pl.semaphore_signal(barrier, inc=1, device_id=who, device_id_type=MESH)

    greet(first_from)
    greet(sibling)
    for step in range(1, X):
        greet(x_peer(step))
    for step in range(1, Y):
        greet(y_peer(step))
    for step in range(1, ZL):
        greet(z_peer(step))
    greet(end_peer(1 - zh))

    @pl.when(jnp.logical_not(home))
    def _():
        greet(end_peer(zh))

    fetch_l.wait()
    for block in range(3):
        rows = pl.ds(block * 128, 128)
        member = mask_ref[0, block].astype(jnp.float32)
        masked[rows, :] = l_ref[rows, :] * member

    pl.semaphore_wait(barrier, jnp.where(home, 16, 17))

    def spot(j, half, part):
        return m.at[j, half, pl.ds(part * (384 // PARTS), 384 // PARTS), :]

    def first(part):
        return copy_to(
            masked.at[pl.ds(part * (384 // PARTS), 384 // PARTS), :],
            spot(first_slot, first_half, part),
            s_first.at[part], r_m.at[first_slot, first_half, part], first_to,
        )

    for part in range(PARTS):
        first(part).start()

    def send_a(piece):
        rows = pl.ds(piece * 128, 128)
        return copy_to(
            a_ref.at[rows, :], a_in.at[rows, :], s_a.at[piece], r_a.at[piece], a_partner
        )

    fetch_a.wait()
    for piece in range(PIECES):
        send_a(piece).start()
    high, low = split(a_ref[...])
    a_high[kind], a_low[kind] = high, low
    high, low = split(masked[...].T)
    turned[0], turned[1] = high, low

    def order(i):
        half = lax.div(i + 1, 2)
        near = jnp.where(lax.rem(i, 2) == 1, zl - half, zl + half)
        far = jnp.where(zl <= 3, i, 7 - i)
        return jnp.where(i <= 2 * jnp.minimum(zl, 7 - zl), near, far)

    def to_right(j, part):
        here = spot(j, mine, part)
        return copy_to(
            here, here, s_right.at[j, part], r_m.at[j, mine, part],
            device(x, jnp.minimum(zl + 1, 7), zh, y, co),
        )

    def to_left(j, part):
        here = spot(j, mine, part)
        return copy_to(
            here, here, s_left.at[j, part], r_m.at[j, mine, part],
            device(x, jnp.maximum(zl - 1, 0), zh, y, co),
        )

    def to_partner(j, part):
        here = spot(j, mine, part)
        return copy_to(here, here, s_x.at[j, part], r_m.at[j, mine, part], partner)

    def arrival(j, half, part):
        here = spot(j, half, part)
        return copy_to(here, here, s_first.at[0], r_m.at[j, half, part], partner)

    def to_sibling(j):
        return copy_to(p.at[j, 1 - co], c.at[j], s_c.at[j], r_c.at[j], sibling)

    def role(j):
        half = 1 - lax.rem(j, 2)
        toward = 1 - 2 * half
        return lax.rem(y - lax.div(j, 2) + Y, Y), half, toward

    def to_owner(j):
        _, half, toward = role(j)
        owner = lax.div(j, 2)
        side = jnp.where(lax.rem(y - owner + Y, Y) == 1, 0, 1)
        return copy_to(
            p.at[j, co], yr.at[half, side], s_y.at[j], r_y.at[half, side],
            device(x, zl, zh, owner, co),
        )

    def to_between(j):
        _, half, toward = role(j)
        return copy_to(
            p.at[j, co], far.at[half], s_y.at[j], r_far.at[half],
            device(x, zl, zh, lax.rem(y - toward + Y, Y), co),
        )

    def to_end(half):
        return copy_to(t.at[half], zb.at[zh], s_z.at[half], r_z.at[zh], end_peer(half))

    def goes_right(j):
        return jnp.logical_and(j <= zl, zl < 7)

    def goes_left(j):
        return jnp.logical_and(j >= zl, zl > 0)

    def step(i, carry):
        def forward(part, now):
            @pl.when(jnp.logical_and(i < 8, now))
            def _():
                j = order(i)
                arrival(j, mine, part).wait_recv()

                @pl.when(goes_right(j))
                def _():
                    to_right(j, part).start()

                @pl.when(goes_left(j))
                def _():
                    to_left(j, part).start()

                to_partner(j, part).start()

        works = jnp.logical_and(i >= LAG, i < LAG + 8)

        def multiply(j, q):
            p[j, q] = product(a_high[q], a_low[q], m[j].reshape(768, 128))

        early = i <= LAG
        forward(0, True)
        forward(1, early)
        forward(2, early)

        @pl.when(i == LAG)
        def _():
            for piece in range(PIECES):
                send_a(piece).wait_recv()
            high, low = split(a_in[...])
            a_high[1 - kind], a_low[1 - kind] = high, low

        @pl.when(works)
        def _():
            j = order(i - LAG)
            for part in range(PARTS):
                arrival(j, 1 - mine, part).wait_recv()
            multiply(j, 1 - co)
            to_sibling(j).start()

        forward(1, i > LAG)

        @pl.when(works)
        def _():
            multiply(order(i - LAG), co)

        forward(2, i > LAG)

        k = i - (LAG + 1)

        @pl.when(jnp.logical_and(k >= 0, k < 8))
        def _():
            j = order(k)
            to_sibling(j).wait_recv()
            p[j, co] = p[j, co] + c[j]

            distance, _, toward = role(j)

            @pl.when(distance == lax.rem(Y - toward, Y))
            def _():
                to_owner(j).start()

            @pl.when(distance == 2)
            def _():
                to_between(j).start()

        @pl.when(jnp.logical_and(k >= PASS, k < PASS + 8))
        def _():
            j = order(k - PASS)
            distance, half, toward = role(j)

            @pl.when(distance == lax.rem(Y + toward, Y))
            def _():
                copy_to(t.at[0], far.at[half], s_y.at[0], r_far.at[half], sibling).wait_recv()
                p[j, co] = p[j, co] + far[half]
                to_owner(j).start()

        @pl.when(jnp.logical_and(k >= TRAIL, k < TRAIL + 8))
        def _():
            j = order(k - TRAIL)
            half = 1 - lax.rem(j, 2)

            @pl.when(lax.div(j, 2) == y)
            def _():
                for slot in range(2):
                    copy_to(
                        t.at[0], yr.at[half, slot], s_y.at[0], r_y.at[half, slot], sibling
                    ).wait_recv()
                total = p[j, co] + (yr[half, 0] + yr[half, 1])
                stays = jnp.logical_and(home, half == zh)

                @pl.when(stays)
                def _():
                    zb[zh] = total

                @pl.when(jnp.logical_not(stays))
                def _():
                    t[half] = total
                    to_end(half).start()

        return carry

    lax.fori_loop(0, 8 + LAG + 1 + TRAIL, step, 0)

    for part in range(PARTS):
        first(part).wait_send()
    for piece in range(PIECES):
        send_a(piece).wait_send()

    def finish(j, carry):
        to_sibling(j).wait_send()
        for part in range(PARTS):
            to_partner(j, part).wait_send()

            @pl.when(goes_right(j))
            def _(part=part):
                to_right(j, part).wait_send()

            @pl.when(goes_left(j))
            def _(part=part):
                to_left(j, part).wait_send()

        distance, _, _ = role(j)

        @pl.when(distance == 2)
        def _():
            to_between(j).wait_send()

        @pl.when(lax.rem(distance, 2) == 1)
        def _():
            to_owner(j).wait_send()

        return carry

    lax.fori_loop(0, 8, finish, 0)

    def end_arrival(half):
        return copy_to(t.at[0], zb.at[half], s_z.at[0], r_z.at[half], sibling)

    end_arrival(1 - zh).wait_recv()

    @pl.when(jnp.logical_not(home))
    def _():
        end_arrival(zh).wait_recv()

    for block in range(3):
        rows = pl.ds(block * 128, 128)
        member = mask_ref[0, block].astype(jnp.float32)
        off_ref[rows, :] = -((zb[0, rows, :] + zb[1, rows, :]) * member)

    correction = product(turned[0], turned[1], off_ref[...])
    for other in range(X):
        cs[other] = correction[other * 32 : other * 32 + 32, :]

    def corr_x(step):
        return copy_to(
            cs.at[lax.rem(x + step, X)], cx.at[step - 1], s_cx.at[step - 1], r_cx.at[step - 1],
            x_peer(step),
        )

    def corr_z(step):
        return copy_to(cz.at[zl], cz.at[zl], s_cz.at[step - 1], r_cz.at[zl], z_peer(step))

    def corr_back(step):
        return copy_to(dg.at[x], dg.at[x], s_dg.at[step - 1], r_dg.at[x], x_peer(step))

    for step_ in range(1, X):
        corr_x(step_).start()
    for step_ in range(1, X):
        corr_x(step_).wait_recv()
    cz[zl] = (cs[x] + cx[0]) + (cx[1] + cx[2])
    for step_ in range(1, ZL):
        corr_z(step_).start()
    for step_ in range(1, ZL):
        other = lax.rem(zl + step_, ZL)
        copy_to(cz.at[other], cz.at[other], s_cz.at[0], r_cz.at[other], sibling).wait_recv()
    dg[x] = ((cz[0] + cz[1]) + (cz[2] + cz[3])) + ((cz[4] + cz[5]) + (cz[6] + cz[7]))
    for step_ in range(1, X):
        corr_back(step_).start()
    for step_ in range(1, X):
        other = lax.rem(x + step_, X)
        copy_to(dg.at[other], dg.at[other], s_dg.at[0], r_dg.at[other], sibling).wait_recv()
    fetch_dinv.wait()
    for other in range(X):
        rows = pl.ds(other * 32, 32)
        diag_ref[0, rows, :] = dinv_ref[0, rows, :] - dg[other]

    to_end(1 - zh).wait_send()

    @pl.when(jnp.logical_not(home))
    def _():
        to_end(zh).wait_send()

    for step_ in range(1, X):
        corr_x(step_).wait_send()
        corr_back(step_).wait_send()
    for step_ in range(1, ZL):
        corr_z(step_).wait_send()


def on_device(inverse_part, lower_panel, struct_mask, diag_inverse):
    f32, bf16 = jnp.float32, jnp.bfloat16
    dma = pltpu.SemaphoreType.DMA
    hbm = pl.BlockSpec(memory_space=pl.ANY)
    vmem = pl.BlockSpec(memory_space=pltpu.VMEM)
    return tuple(
        pl.pallas_call(
            kernel,
            out_shape=(
                jax.ShapeDtypeStruct((384, 128), f32),
                jax.ShapeDtypeStruct((1, 128, 128), f32),
            ),
            in_specs=[hbm, hbm, pl.BlockSpec(memory_space=pltpu.SMEM), hbm],
            out_specs=(vmem, vmem),
            scratch_shapes=[
                pltpu.VMEM((384, 768), f32),
                pltpu.VMEM((384, 128), f32),
                pltpu.VMEM((1, 128, 128), f32),
                pltpu.VMEM((384, 128), f32),
                pltpu.VMEM((2, 128, 384), bf16),
                pltpu.VMEM((384, 768), f32),
                pltpu.VMEM((2, 384, 768), bf16),
                pltpu.VMEM((2, 384, 768), bf16),
                pltpu.VMEM((8, 2, 384, 128), f32),
                pltpu.VMEM((8, 2, 384, 128), f32),
                pltpu.VMEM((8, 384, 128), f32),
                pltpu.VMEM((2, 384, 128), f32),
                pltpu.VMEM((2, 2, 384, 128), f32),
                pltpu.VMEM((2, 384, 128), f32),
                pltpu.VMEM((2, 384, 128), f32),
                pltpu.VMEM((4, 32, 128), f32),
                pltpu.VMEM((3, 32, 128), f32),
                pltpu.VMEM((8, 32, 128), f32),
                pltpu.VMEM((4, 32, 128), f32),
                dma((3,)), dma((PIECES,)), dma((PIECES,)), dma((PARTS,)),
                dma((8, PARTS)), dma((8, PARTS)), dma((8, PARTS)), dma((8, 2, PARTS)),
                dma((8,)), dma((8,)), dma((8,)), dma((2, 2)), dma((2,)), dma((2,)), dma((2,)),
                dma((3,)), dma((3,)), dma((7,)), dma((8,)), dma((3,)), dma((4,)),
            ],
            compiler_params=pltpu.CompilerParams(
                collective_id=0, has_side_effects=True, vmem_limit_bytes=63 * 1024 * 1024
            ),
            cost_estimate=pl.CostEstimate(
                flops=2 * 3 * 384 * 768 * 2048, bytes_accessed=4_000_000, transcendentals=0
            ),
        )(inverse_part, lower_panel, struct_mask, diag_inverse)
    )


def solution(mesh):
    return jax.shard_map(
        on_device,
        mesh=mesh,
        in_specs=(P("prow", "pcol"), P("prow", "pcol"), P("pcol", "prow"), P("pcol", None, None)),
        out_specs=(P("prow", "pcol"), P("pcol", None, None)),
        check_vma=False,
    )
```
